32 devices in a mesh: row: 4 (over y, core), col: 8 (over z, x).
Axes of the slice: x: 2, y: 2, z: 4, core: 2. Of those that a mesh axis runs over, the one named last changes fastest.
Arguments:
- features: bfloat16 [4096, 128], P('col', 'row'), may hold values from -6 to 6
- weight: bfloat16 [128, 128], replicated, may hold values from -0.5 to 0.5
- bias_vector: float32 [128], replicated, may hold values from -3 to 3
- tile_rows: int32 [4, 8, 128], P('row', 'col'), may hold values from 0 to 7
- tile_cols: int32 [4, 8, 128], P('row', 'col'), may hold values from 0 to 3
- neighbours: int32 [4, 8, 128, 2, 128], P('row', 'col'), may hold values from 0 to 127, as said below
- edge_weights: bfloat16 [4, 8, 128, 2, 128], P('row', 'col'), may hold values from 0.039794922 to 0.3984375
- tile_count: int32 [4, 8], P('row', 'col'), may hold values from 16 to 128, as said below
- cotangent: float32 [4096, 128], P(('row', 'col')), may hold values from -6 to 6
Outputs:
- activations: float32 [4096, 128], P(('row', 'col'))
- grad_features: bfloat16 [4096, 128], P('col', 'row')
- grad_weight: float32 [128, 128], replicated
- grad_bias: float32 [128], replicated
The draws below stay inside these ranges and needn't reach their ends.
Inputs may be any that keep to these rules, and one draw needn't show every extreme that they name: `tile_count`: one device uses all 128 tile slots in every draw. The 2 neighbours of one galaxy within one tile are distinct.
All inputs are finite; a program needn't handle non-finite values.
Results may differ from the reference program's by a relative error of at most 0.006.
Values may be sent and summed in bfloat16 or wider, within the bound.
No kernel may reach another device: no remote copies, remote signals or barrier semaphores. Data moves between devices by JAX's collectives and lax.ppermute only.
A program may use at most 64 MiB of HBM per device.

```python
import math
import jax
import jax.numpy as jnp
from jax import lax

HID = 128
TILE = 128
NBR = 2
TILE_MAX = 128
ROW_BLOCKS = 8
COL_BLOCKS = 4
NODES = 4096
N_ROW = 4
N_COL = 8


def draw_neighbours(key, part):
    window_span = TILE // NBR
    full_shape = (N_ROW, N_COL, TILE_MAX, NBR, TILE)
    offsets = jax.random.randint(jax.random.fold_in(key, 11), full_shape, 0, window_span)
    rotation = jax.random.randint(jax.random.fold_in(key, 12), (N_ROW, N_COL, TILE_MAX, 1, TILE), 0, TILE)
    lane_start = jnp.arange(NBR, dtype=jnp.int32).reshape(1, 1, 1, NBR, 1) * window_span
    return ((offsets + lane_start + rotation) % TILE).astype(jnp.int32)


def draw_tile_count(key, part):
    counts = jax.random.randint(jax.random.fold_in(key, 21), (N_ROW * N_COL,), TILE_MAX // 8, 3 * TILE_MAX // 8 + 1)
    chosen = jax.random.randint(jax.random.fold_in(key, 22), (), 0, N_ROW * N_COL)
    device_ids = jnp.arange(N_ROW * N_COL, dtype=jnp.int32)
    counts = jnp.where(device_ids == chosen, TILE_MAX, counts)
    return counts.reshape(N_ROW, N_COL).astype(jnp.int32)


def with_ends(values, own_key, least, top_value):
    index_at = [jax.random.randint(jax.random.fold_in(own_key, axis), (), 0, length) for axis, length in enumerate(values.shape)]
    main_axis = values.shape.index(max(values.shape))
    beside = index_at[:main_axis] + [(index_at[main_axis] + 1) % values.shape[main_axis]] + index_at[main_axis + 1:]
    return values.at[tuple(index_at)].set(least).at[tuple(beside)].set(top_value)


def level_of(own_key, dims, cuts, smallest, high):
    gain = 1.0
    for position, shards_of in cuts:
        draws = jax.random.uniform(jax.random.fold_in(jax.random.fold_in(own_key, 6), position), (shards_of,), jnp.float32, smallest / len(cuts), high / len(cuts))
        gain = gain * jnp.repeat(jnp.exp(draws), dims[position] // shards_of).reshape((-1,) + (1,) * (len(dims) - 1 - position))
    return gain


def normal_values(own_key, extent, width, limit, shards=(), kind=jnp.bfloat16):
    entries = jax.random.normal(own_key, extent, jnp.float32) * width
    if len(shards) > 0:
        entries = level_of(own_key, extent, shards, -0.22, 0.18) * entries
    return jnp.clip(entries, min=-limit, max=limit).astype(kind)


def setup_inputs(seed: int = 0) -> dict:
    arg_keys = jax.random.split(jax.random.key(seed), 10)
    features = normal_values(arg_keys[0], (NODES, HID), 1.0, 6.0, ((0, 8), (1, 4)))
    weight = normal_values(arg_keys[1], (HID, HID), HID ** -0.5, 0.5)
    bias_vector = normal_values(arg_keys[2], (HID,), 0.5, 3.0, (), jnp.float32)
    tile_rows = with_ends(jax.random.randint(arg_keys[3], (N_ROW, N_COL, TILE_MAX), 0, ROW_BLOCKS), jax.random.fold_in(arg_keys[3], 1), 0, ROW_BLOCKS - 1).astype(jnp.int32)
    tile_cols = with_ends(jax.random.randint(arg_keys[4], (N_ROW, N_COL, TILE_MAX), 0, COL_BLOCKS), jax.random.fold_in(arg_keys[4], 1), 0, COL_BLOCKS - 1).astype(jnp.int32)
    neighbours = draw_neighbours(jax.random.fold_in(arg_keys[9], 71), 0)
    edge_weights = jnp.clip(jnp.exp(math.log(0.3984375) - 2.3038113 * jax.random.uniform(arg_keys[6], (N_ROW, N_COL, TILE_MAX, NBR, TILE), jnp.float32) ** level_of(arg_keys[6], (N_ROW, N_COL, TILE_MAX, NBR, TILE), ((0, 4), (1, 8)), -0.2, 0.2)), 0.039794922, 0.3984375).astype(jnp.bfloat16)
    tile_count = draw_tile_count(jax.random.fold_in(arg_keys[9], 71), 0)
    cotangent = normal_values(arg_keys[8], (NODES, HID), 1.0, 6.0, ((0, 32),), jnp.float32)
    return dict(features=features, weight=weight, bias_vector=bias_vector, tile_rows=tile_rows, tile_cols=tile_cols, neighbours=neighbours, edge_weights=edge_weights, tile_count=tile_count, cotangent=cotangent)


def edge_lists(tile_rows, tile_cols, neighbours, edge_weights, tile_count, node_count):
    row_nodes = node_count // N_ROW
    col_nodes = node_count // N_COL
    slot_ids = jnp.arange(TILE_MAX, dtype=jnp.int32).reshape(1, 1, TILE_MAX)
    live_slot = slot_ids < tile_count[:, :, None]
    row_owner = jnp.arange(N_ROW, dtype=jnp.int32).reshape(N_ROW, 1, 1) * row_nodes
    col_owner = jnp.arange(N_COL, dtype=jnp.int32).reshape(1, N_COL, 1) * col_nodes
    row_first = row_owner + tile_rows * TILE
    col_first = col_owner + tile_cols * TILE
    galaxy = jnp.arange(TILE, dtype=jnp.int32).reshape(1, 1, 1, 1, TILE)
    targets = row_first[:, :, :, None, None] + galaxy + jnp.zeros_like(neighbours)
    sources = col_first[:, :, :, None, None] + neighbours
    values = jnp.where(live_slot[:, :, :, None, None], edge_weights.astype(jnp.float32), jnp.zeros((), jnp.float32))
    pairs_total = N_ROW * N_COL
    return targets.reshape(pairs_total, -1), sources.reshape(pairs_total, -1), values.reshape(pairs_total, -1)


def spread(source_rows, targets, sources, values, node_count):
    def accumulate(summed, edge_block):
        target, source, weight_row = edge_block
        summed = summed.at[target].add(weight_row[:, None] * source_rows[source].astype(jnp.float32))
        return summed, None

    zeroes = jnp.zeros((node_count, source_rows.shape[1]), jnp.float32)
    summed, _ = lax.scan(accumulate, zeroes, (targets, sources, values))
    return summed


def reference(features, weight, bias_vector, tile_rows, tile_cols, neighbours, edge_weights, tile_count, cotangent):
    node_count = features.shape[0]
    targets, sources, values = edge_lists(tile_rows, tile_cols, neighbours, edge_weights, tile_count, node_count)
    projected = jnp.dot(features, weight, preferred_element_type=jnp.float32).astype(jnp.bfloat16)
    pre = spread(projected, targets, sources, values, node_count) + bias_vector
    squashed = jax.nn.sigmoid(pre)
    activations = pre * squashed
    pre_grad = (cotangent * squashed * (1.0 + pre * (1.0 - squashed))).astype(jnp.bfloat16)
    proj_grad = spread(pre_grad, sources, targets, values, node_count)
    shrink = float(node_count) ** -0.5
    weight_wide = weight.astype(jnp.float32)
    grad_features = jnp.dot(proj_grad, weight_wide.T, precision=lax.Precision.HIGHEST).astype(jnp.bfloat16)
    grad_weight = jnp.dot(features.astype(jnp.float32).T, proj_grad, precision=lax.Precision.HIGHEST) * shrink
    grad_bias = jnp.sum(pre_grad.astype(jnp.float32), axis=0) * shrink
    return activations, grad_features, grad_weight, grad_bias
```

```python
import functools

import jax
import jax.numpy as jnp
from jax import lax
from jax.experimental import pallas as pl
from jax.experimental.pallas import tpu as pltpu
from jax.sharding import PartitionSpec as P

f32 = jnp.float32
bf16 = jnp.bfloat16
tail = 16
wide = 1024
grant = 8 * 2**20


def room(*arrays):
    size = sum(a.size * a.dtype.itemsize for a in arrays)
    return pltpu.CompilerParams(vmem_limit_bytes=grant + 2 * size)


def vmem():
    return pl.BlockSpec(memory_space=pltpu.VMEM)


def smem():
    return pl.BlockSpec(memory_space=pltpu.SMEM)


def struct(shape, dtype):
    return jax.ShapeDtypeStruct(shape, dtype)


def dims(left, right):
    return (((left,), (right,)), ((), ()))


def dot(a, b, left=1, right=0):
    return lax.dot_general(a, b, dims(left, right), preferred_element_type=f32)


def each(count, body):
    if count <= 64:
        for index in range(count):
            body(index)
    else:
        lax.fori_loop(0, count, lambda index, none: (body(index), none)[1], 0)


def start_of(index, size):
    return index * size if isinstance(index, int) else pl.multiple_of(index * size, size)


def partner(me, step, size):
    if size & (size - 1) == 0:
        return me ^ step
    return (me + step) % size


def source(me, step, size):
    if size & (size - 1) == 0:
        return me ^ step
    return (me + size - step) % size


def exchange(value, axis, step):
    size = lax.axis_size(axis)
    return lax.ppermute(value, axis, [(i, partner(i, step, size)) for i in range(size)])


def band_kernel(limit, rows, cols, ids, values, band, sums, scaled):
    blocks, tile, _ = sums.shape
    row_blocks = band.shape[1] // tile
    slots = rows.shape[-1]
    lanes = ids.shape[0] // slots

    def clear(index):
        sums[index] = jnp.zeros((tile, tile), f32)

    each(blocks, clear)
    scaled[...] = values[...].astype(f32)
    which = lax.broadcasted_iota(jnp.int32, (tile, tile), 0)

    def add(slot, none):
        block = cols[0, 0, slot] * row_blocks + rows[0, 0, slot]
        dense = sums[block]
        for lane in range(lanes):
            line = pl.ds(slot * lanes + lane, 1)
            dense = dense + jnp.where(which == ids[line, :], scaled[line, :], 0.0)
        sums[block] = dense
        return none

    lax.fori_loop(0, limit[0, 0], add, 0)

    def put(index):
        col, row = index // row_blocks, index % row_blocks
        band[pl.ds(start_of(col, tile), tile), pl.ds(start_of(row, tile), tile)] = sums[index].astype(bf16)

    each(blocks, put)


def make_band(limit, rows, cols, ids, values, row_blocks, col_blocks):
    tile = ids.shape[-1]
    lines = ids.shape[-3] * ids.shape[-2]
    ids = ids.reshape(lines, tile)
    values = values.reshape(lines, tile)
    out = struct((col_blocks * tile, row_blocks * tile), bf16)
    sums = struct((col_blocks * row_blocks, tile, tile), f32)
    return pl.pallas_call(
        band_kernel,
        out_shape=out,
        in_specs=[smem(), smem(), smem(), vmem(), vmem()],
        out_specs=vmem(),
        scratch_shapes=[pltpu.VMEM(sums.shape, f32), pltpu.VMEM((lines, tile), f32)],
        compiler_params=pltpu.CompilerParams(vmem_limit_bytes=grant + sums.size * 4 + out.size * 2),
        cost_estimate=pl.CostEstimate(flops=8 * sums.size * 8, bytes_accessed=8 * 2**20, transcendentals=0),
        name="band",
    )(limit, rows, cols, ids, values)


def forward_kernel(size, owners, *refs):
    parts, (band, out, panel) = refs[:size], refs[size:]
    me = lax.axis_index("row")
    width = parts[0].shape[0]
    for step, part in enumerate(parts):
        slot = pl.multiple_of(source(me, step, size) * width, width)
        panel[pl.ds(slot, width), :] = part[...].astype(f32)
    left = panel[...].astype(bf16)
    own = out.shape[2]
    many = min(wide, band.shape[1])

    def piece(index):
        got = dot(left, band[:, pl.ds(start_of(index, many), many)]).astype(bf16)
        for part in range(many // own):
            out[index * (many // own) + part] = got[:, part * own : (part + 1) * own]

    each(band.shape[1] // many, piece)


def forward(parts, band, owners):
    hidden = parts[0].shape[0] * len(parts)
    nodes, total = band.shape
    return pl.pallas_call(
        functools.partial(forward_kernel, len(parts), owners),
        out_shape=struct((owners, hidden, total // owners), bf16),
        in_specs=[vmem()] * (len(parts) + 1),
        out_specs=vmem(),
        scratch_shapes=[pltpu.VMEM((hidden, nodes), f32)],
        compiler_params=room(band),
        name="forward",
    )(*parts, band)


def pair_rows(line):
    high = line.astype(bf16).astype(f32)
    row = lax.broadcasted_iota(jnp.int32, (tail, line.shape[1]), 0)
    return jnp.where(row == 0, high, jnp.where(row == 1, line - high, 0.0))


def own_kernel(got, weight, bias, cotangent, act, message):
    owners, hidden, own = got.shape
    total = got[0].astype(f32)
    for index in range(1, owners):
        total = total + got[index].astype(f32)
    high = total.astype(bf16)
    low = (total - high.astype(f32)).astype(bf16)
    pre = dot(high, weight[...], 0, 0) + dot(low, weight[...], 0, 0) + bias[...]
    squashed = jax.nn.sigmoid(pre)
    act[...] = pre * squashed
    grad = cotangent[...] * squashed * (1.0 + pre * (1.0 - squashed))
    grad = grad.astype(bf16)
    back = dot(weight[...], grad, 1, 1).astype(bf16)
    weight_part = dot(high, grad).astype(bf16)
    bias_part = pair_rows(jnp.sum(grad.astype(f32), axis=0, keepdims=True)).astype(bf16)
    for index in range(owners):
        message[index, :hidden, :] = back
        message[index, hidden : 2 * hidden, :] = weight_part
        message[index, 2 * hidden :, :] = bias_part


def own_rows(got, weight, bias, cotangent):
    owners, hidden, own = got.shape
    return pl.pallas_call(
        own_kernel,
        out_shape=(struct(cotangent.shape, f32), struct((owners, 2 * hidden + tail, own), bf16)),
        in_specs=[vmem()] * 4,
        out_specs=(vmem(), vmem()),
        compiler_params=room(got),
        name="own_rows",
    )(got, weight, bias.reshape(1, hidden), cotangent)


def backward_kernel(size, got, band, *refs):
    messages, (kept, wide_rows, grads, packed) = refs[:size], refs[size:]
    owners, _, own = got.shape
    hidden = kept.shape[0] * size
    width, nodes = kept.shape
    me = lax.axis_index("row")
    weight_part = jnp.zeros((hidden, own), f32)
    bias_part = jnp.zeros((1, own), f32)
    for index in range(owners):
        wide_rows[:, index * own : (index + 1) * own] = got[index, :hidden, :]
        weight_part = weight_part + got[index, hidden : 2 * hidden, :].astype(f32)
        bias_part = bias_part + jnp.sum(got[index, 2 * hidden :, :].astype(f32), axis=0, keepdims=True)
    many = min(wide, nodes)

    def piece(index):
        place = pl.ds(start_of(index, many), many)
        grads[:, place] = dot(wide_rows[...], band[place, :], 1, 1)

    each(nodes // many, piece)
    per_row = nodes // own
    for part in range(hidden // width):
        packed[width : 2 * width, part * own : (part + 1) * own] = weight_part[part * width : (part + 1) * width]
    packed[2 * width :, :] = jnp.zeros((tail, nodes), f32)
    packed[2 * width :, :own] = pair_rows(bias_part)
    for step in range(size):
        slot = pl.multiple_of(partner(me, step, size) * width, width)
        block = grads[pl.ds(slot, width), :]
        if step == 0:
            kept[...] = block
        packed[:width, :] = block
        messages[step][...] = packed[...].astype(bf16)


def backward(got, band, size):
    owners, _, own = got.shape
    nodes, total = band.shape
    hidden = (got.shape[1] - tail) // 2
    width = hidden // size
    message = struct((2 * width + tail, nodes), bf16)
    return pl.pallas_call(
        functools.partial(backward_kernel, size),
        out_shape=(message,) * size + (struct((width, nodes), f32),),
        in_specs=[vmem()] * 2,
        out_specs=(vmem(),) * (size + 1),
        scratch_shapes=[
            pltpu.VMEM((hidden, total), bf16),
            pltpu.VMEM((hidden, nodes), f32),
            pltpu.VMEM((2 * width + tail, nodes), f32),
        ],
        compiler_params=room(band, got),
        name="backward",
    )(got, band)


def final_kernel(size, shrink, *refs):
    messages, (kept, features, weight, bias, slots) = refs[:size], refs[size:]
    width, nodes = kept.shape
    hidden = weight.shape[0]
    me = lax.axis_index("row")
    total = kept[...]
    for step, message in enumerate(messages):
        whole = message[...].astype(f32)
        if step > 0:
            total = total + whole[:width]
        slots[source(me, step, size)] = whole[width:]
    features[...] = total.T.astype(bf16)
    summed = slots[0]
    for index in range(1, size):
        summed = summed + slots[index]
    summed = summed * shrink
    for part in range(hidden // width):
        weight[part * width : (part + 1) * width, :] = summed[:width, part * hidden : (part + 1) * hidden]
    bias[...] = summed[width : width + 1, :hidden] + summed[width + 1 : width + 2, :hidden]


def final(messages, kept, hidden, shrink):
    width, nodes = kept.shape
    size = len(messages)
    return pl.pallas_call(
        functools.partial(final_kernel, size, shrink),
        out_shape=(struct((nodes, width), bf16), struct((hidden, hidden), f32), struct((1, hidden), f32)),
        in_specs=[vmem()] * (size + 1),
        out_specs=(vmem(),) * 3,
        scratch_shapes=[pltpu.VMEM((size, width + tail, nodes), f32)],
        compiler_params=room(*messages),
        name="final",
    )(*messages, kept)


def shards(
    features,
    weight,
    bias_vector,
    tile_rows,
    tile_cols,
    neighbours,
    edge_weights,
    tile_count,
    cotangent,
):
    tile_size = neighbours.shape[-1]
    hidden = weight.shape[1]
    size, owners = lax.axis_size("row"), lax.axis_size("col")
    blocks_own = cotangent.shape[0] // tile_size
    row_blocks = blocks_own * owners
    col_blocks = blocks_own * size
    turned = features.T
    parts = [turned] + [exchange(turned, "row", step) for step in range(1, size)]
    band = make_band(tile_count, tile_rows, tile_cols, neighbours, edge_weights, row_blocks, col_blocks)
    sums = forward(parts, band, owners)
    sums = lax.all_to_all(sums, "col", 0, 0, tiled=True)
    activations, message = own_rows(sums, weight, bias_vector, cotangent)
    message = lax.all_to_all(message, "col", 0, 0, tiled=True)
    *messages, kept = backward(message, band, size)
    messages = [messages[0]] + [exchange(messages[step], "row", step) for step in range(1, size)]
    node_count = cotangent.shape[0] * size * owners
    grad_features, grad_weight, grad_bias = final(messages, kept, hidden, float(node_count) ** (-0.5))
    return (activations, grad_features, grad_weight, grad_bias.reshape(hidden))


def solution(mesh):
    in_specs = (
        P("col", "row"),
        P(),
        P(),
        P("row", "col", None),
        P("row", "col", None),
        P("row", "col", None, None, None),
        P("row", "col", None, None, None),
        P("row", "col"),
        P(("row", "col"), None),
    )
    out_specs = (P(("row", "col"), None), P("col", "row"), P(), P())
    return jax.shard_map(shards, mesh=mesh, in_specs=in_specs, out_specs=out_specs, check_vma=False)
```

```python
import functools

import jax
import jax.numpy as jnp
from jax import lax
from jax.experimental import pallas as pl
from jax.experimental.pallas import tpu as pltpu
from jax.sharding import PartitionSpec as P

f32 = jnp.float32
bf16 = jnp.bfloat16
tail = 16
wide = 1024
grant = 8 * 2**20


def room(*arrays):
    size = sum(a.size * a.dtype.itemsize for a in arrays)
    return pltpu.CompilerParams(vmem_limit_bytes=grant + 2 * size)


def vmem():
    return pl.BlockSpec(memory_space=pltpu.VMEM)


def smem():
    return pl.BlockSpec(memory_space=pltpu.SMEM)


def struct(shape, dtype):
    return jax.ShapeDtypeStruct(shape, dtype)


def dims(left, right):
    return (((left,), (right,)), ((), ()))


def dot(a, b, left=1, right=0):
    return lax.dot_general(a, b, dims(left, right), preferred_element_type=f32)


def each(count, body):
    if count <= 64:
        for index in range(count):
            body(index)
    else:
        lax.fori_loop(0, count, lambda index, none: (body(index), none)[1], 0)


def start_of(index, size):
    return index * size if isinstance(index, int) else pl.multiple_of(index * size, size)


def partner(me, step, size):
    if size & (size - 1) == 0:
        return me ^ step
    return (me + step) % size


def source(me, step, size):
    if size & (size - 1) == 0:
        return me ^ step
    return (me + size - step) % size


def exchange(value, axis, step):
    size = lax.axis_size(axis)
    return lax.ppermute(value, axis, [(i, partner(i, step, size)) for i in range(size)])


def band_kernel(limit, rows, cols, ids, values, bias, band, bias_out, sums, scaled, here, row, col, sems):
    blocks, tile, _ = sums.shape
    row_blocks = band.shape[1] // tile
    slots = rows.shape[-1]
    ids_here, values_here = here
    lanes = ids_here.shape[0] // slots
    pairs = ((ids, ids_here), (values, values_here), (rows, row), (cols, col), (bias, bias_out))
    copies = [pltpu.make_async_copy(a, b, sems.at[i]) for i, (a, b) in enumerate(pairs)]
    for copy in copies:
        copy.start()

    def clear(index):
        sums[index] = jnp.zeros((tile, tile), f32)

    each(blocks, clear)
    for copy in copies:
        copy.wait()
    scaled[...] = values_here[...].astype(f32)
    which = lax.broadcasted_iota(jnp.int32, (tile, tile), 0)

    def add(slot, none):
        block = col[0, 0, slot] * row_blocks + row[0, 0, slot]
        dense = sums[block]
        for lane in range(lanes):
            line = pl.ds(slot * lanes + lane, 1)
            dense = dense + jnp.where(which == ids_here[line, :], scaled[line, :], 0.0)
        sums[block] = dense
        return none

    lax.fori_loop(0, limit[0, 0], add, 0)

    def put(index):
        c, r = index // row_blocks, index % row_blocks
        band[pl.ds(start_of(c, tile), tile), pl.ds(start_of(r, tile), tile)] = sums[index].astype(bf16)

    each(blocks, put)


def make_band(limit, rows, cols, ids, values, bias, row_blocks, col_blocks):
    tile = ids.shape[-1]
    lines = ids.shape[-3] * ids.shape[-2]
    ids = ids.reshape(lines, tile)
    values = values.reshape(lines, tile)
    bias = bias.reshape(1, -1)
    out = struct((col_blocks * tile, row_blocks * tile), bf16)
    sums = struct((col_blocks * row_blocks, tile, tile), f32)
    return pl.pallas_call(
        band_kernel,
        out_shape=(out, struct(bias.shape, f32)),
        in_specs=[smem()] + [pl.BlockSpec(memory_space=pltpu.HBM)] * 5,
        out_specs=(vmem(), vmem()),
        scratch_shapes=[
            pltpu.VMEM(sums.shape, f32),
            pltpu.VMEM((lines, tile), f32),
            (pltpu.VMEM((lines, tile), jnp.int32), pltpu.VMEM((lines, tile), bf16)),
            pltpu.SMEM(rows.shape, jnp.int32),
            pltpu.SMEM(cols.shape, jnp.int32),
            pltpu.SemaphoreType.DMA((5,)),
        ],
        compiler_params=pltpu.CompilerParams(vmem_limit_bytes=grant + sums.size * 4 + out.size * 2),
        cost_estimate=pl.CostEstimate(flops=8 * sums.size * 8, bytes_accessed=8 * 2**20, transcendentals=0),
        name="band",
    )(limit, *[pltpu.with_memory_space_constraint(a, pltpu.HBM) for a in (rows, cols, ids, values, bias)])


def forward_kernel(size, owners, *refs):
    parts, (band, out, panel) = refs[:size], refs[size:]
    me = lax.axis_index("row")
    width = parts[0].shape[0]
    for step, part in enumerate(parts):
        slot = pl.multiple_of(source(me, step, size) * width, width)
        panel[pl.ds(slot, width), :] = part[...].astype(f32)
    left = panel[...].astype(bf16)
    own = out.shape[2]
    many = min(wide, band.shape[1])

    def piece(index):
        got = dot(left, band[:, pl.ds(start_of(index, many), many)]).astype(bf16)
        for part in range(many // own):
            out[index * (many // own) + part] = got[:, part * own : (part + 1) * own]

    each(band.shape[1] // many, piece)


def forward(parts, band, owners):
    hidden = parts[0].shape[0] * len(parts)
    nodes, total = band.shape
    return pl.pallas_call(
        functools.partial(forward_kernel, len(parts), owners),
        out_shape=struct((owners, hidden, total // owners), bf16),
        in_specs=[vmem()] * (len(parts) + 1),
        out_specs=vmem(),
        scratch_shapes=[pltpu.VMEM((hidden, nodes), f32)],
        compiler_params=room(band),
        name="forward",
    )(*parts, band)


def pair_rows(line):
    high = line.astype(bf16).astype(f32)
    row = lax.broadcasted_iota(jnp.int32, (tail, line.shape[1]), 0)
    return jnp.where(row == 0, high, jnp.where(row == 1, line - high, 0.0))


def own_kernel(got, weight, bias, cotangent, act, message):
    owners, hidden, own = got.shape
    total = got[0].astype(f32)
    for index in range(1, owners):
        total = total + got[index].astype(f32)
    high = total.astype(bf16)
    low = (total - high.astype(f32)).astype(bf16)
    pre = dot(high, weight[...], 0, 0) + dot(low, weight[...], 0, 0) + bias[...]
    squashed = jax.nn.sigmoid(pre)
    act[...] = pre * squashed
    grad = cotangent[...] * squashed * (1.0 + pre * (1.0 - squashed))
    grad = grad.astype(bf16)
    back = dot(weight[...], grad, 1, 1).astype(bf16)
    weight_part = (dot(high, grad) + dot(low, grad)).astype(bf16)
    bias_part = pair_rows(jnp.sum(grad.astype(f32), axis=0, keepdims=True)).astype(bf16)
    for index in range(owners):
        message[index, :hidden, :] = back
        message[index, hidden : 2 * hidden, :] = weight_part
        message[index, 2 * hidden :, :] = bias_part


def own_rows(got, weight, bias, cotangent):
    owners, hidden, own = got.shape
    return pl.pallas_call(
        own_kernel,
        out_shape=(struct(cotangent.shape, f32), struct((owners, 2 * hidden + tail, own), bf16)),
        in_specs=[vmem()] * 4,
        out_specs=(vmem(), vmem()),
        compiler_params=room(got),
        name="own_rows",
    )(got, weight, bias, cotangent)


def backward_kernel(size, got, band, *refs):
    messages, (kept, wide_rows, grads, packed) = refs[:size], refs[size:]
    owners, _, own = got.shape
    hidden = kept.shape[0] * size
    width, nodes = kept.shape
    me = lax.axis_index("row")
    weight_part = jnp.zeros((hidden, own), f32)
    bias_part = jnp.zeros((1, own), f32)
    for index in range(owners):
        wide_rows[:, index * own : (index + 1) * own] = got[index, :hidden, :]
        weight_part = weight_part + got[index, hidden : 2 * hidden, :].astype(f32)
        bias_part = bias_part + jnp.sum(got[index, 2 * hidden :, :].astype(f32), axis=0, keepdims=True)
    many = min(wide, nodes)

    def piece(index):
        place = pl.ds(start_of(index, many), many)
        grads[:, place] = dot(wide_rows[...], band[place, :], 1, 1)

    each(nodes // many, piece)
    per_row = nodes // own
    for part in range(hidden // width):
        packed[width : 2 * width, part * own : (part + 1) * own] = weight_part[part * width : (part + 1) * width]
    packed[2 * width :, :] = jnp.zeros((tail, nodes), f32)
    packed[2 * width :, :own] = pair_rows(bias_part)
    for step in range(size):
        slot = pl.multiple_of(partner(me, step, size) * width, width)
        block = grads[pl.ds(slot, width), :]
        if step == 0:
            kept[...] = block
        packed[:width, :] = block
        messages[step][...] = packed[...].astype(bf16)


def backward(got, band, size):
    owners, _, own = got.shape
    nodes, total = band.shape
    hidden = (got.shape[1] - tail) // 2
    width = hidden // size
    message = struct((2 * width + tail, nodes), bf16)
    return pl.pallas_call(
        functools.partial(backward_kernel, size),
        out_shape=(message,) * size + (struct((width, nodes), f32),),
        in_specs=[vmem()] * 2,
        out_specs=(vmem(),) * (size + 1),
        scratch_shapes=[
            pltpu.VMEM((hidden, total), bf16),
            pltpu.VMEM((hidden, nodes), f32),
            pltpu.VMEM((2 * width + tail, nodes), f32),
        ],
        compiler_params=room(band, got),
        name="backward",
    )(got, band)


def final_kernel(size, shrink, *refs):
    messages, (kept, features, weight, bias, slots) = refs[:size], refs[size:]
    width, nodes = kept.shape
    hidden = weight.shape[0]
    me = lax.axis_index("row")
    total = kept[...]
    for step, message in enumerate(messages):
        whole = message[...].astype(f32)
        if step > 0:
            total = total + whole[:width]
        slots[source(me, step, size)] = whole[width:]
    features[...] = total.astype(bf16)
    summed = slots[0]
    for index in range(1, size):
        summed = summed + slots[index]
    summed = summed * shrink
    for part in range(hidden // width):
        weight[part * width : (part + 1) * width, :] = summed[:width, part * hidden : (part + 1) * hidden]
    bias[...] = summed[width : width + 1, :hidden] + summed[width + 1 : width + 2, :hidden]


def final(messages, kept, hidden, shrink):
    width, nodes = kept.shape
    size = len(messages)
    return pl.pallas_call(
        functools.partial(final_kernel, size, shrink),
        out_shape=(struct((width, nodes), bf16), struct((hidden, hidden), f32), struct((1, hidden), f32)),
        in_specs=[vmem()] * (size + 1),
        out_specs=(vmem(),) * 3,
        scratch_shapes=[pltpu.VMEM((size, width + tail, nodes), f32)],
        compiler_params=room(*messages),
        name="final",
    )(*messages, kept)


def shards(
    features,
    weight,
    bias_vector,
    tile_rows,
    tile_cols,
    neighbours,
    edge_weights,
    tile_count,
    cotangent,
):
    tile_size = neighbours.shape[-1]
    hidden = weight.shape[1]
    size, owners = lax.axis_size("row"), lax.axis_size("col")
    blocks_own = cotangent.shape[0] // tile_size
    row_blocks = blocks_own * owners
    col_blocks = blocks_own * size
    turned = features.T
    parts = [turned] + [exchange(turned, "row", step) for step in range(1, size)]
    band, bias = make_band(
        tile_count, tile_rows, tile_cols, neighbours, edge_weights, bias_vector, row_blocks, col_blocks
    )
    sums = forward(parts, band, owners)
    sums = lax.all_to_all(sums, "col", 0, 0, tiled=True)
    activations, message = own_rows(sums, weight, bias, cotangent)
    message = lax.all_to_all(message, "col", 0, 0, tiled=True)
    *messages, kept = backward(message, band, size)
    messages = [messages[0]] + [exchange(messages[step], "row", step) for step in range(1, size)]
    node_count = cotangent.shape[0] * size * owners
    grad_features, grad_weight, grad_bias = final(messages, kept, hidden, float(node_count) ** (-0.5))
    return (activations, grad_features.T, grad_weight, grad_bias.reshape(hidden))


def solution(mesh):
    in_specs = (
        P("col", "row"),
        P(),
        P(),
        P("row", "col", None),
        P("row", "col", None),
        P("row", "col", None, None, None),
        P("row", "col", None, None, None),
        P("row", "col"),
        P(("row", "col"), None),
    )
    out_specs = (P(("row", "col"), None), P("col", "row"), P(), P())
    return jax.shard_map(shards, mesh=mesh, in_specs=in_specs, out_specs=out_specs, check_vma=False)
```

```python
import functools

import jax
import jax.numpy as jnp
from jax import lax
from jax.experimental import pallas as pl
from jax.experimental.pallas import tpu as pltpu
from jax.sharding import PartitionSpec as P

f32 = jnp.float32
bf16 = jnp.bfloat16
tail = 16
wide = 1024
grant = 8 * 2**20


def room(*arrays):
    size = sum(a.size * a.dtype.itemsize for a in arrays)
    return pltpu.CompilerParams(vmem_limit_bytes=grant + 2 * size)


def vmem():
    return pl.BlockSpec(memory_space=pltpu.VMEM)


def smem():
    return pl.BlockSpec(memory_space=pltpu.SMEM)


def struct(shape, dtype):
    return jax.ShapeDtypeStruct(shape, dtype)


def dims(left, right):
    return (((left,), (right,)), ((), ()))


def dot(a, b, left=1, right=0):
    return lax.dot_general(a, b, dims(left, right), preferred_element_type=f32)


def each(count, body):
    if count <= 64:
        for index in range(count):
            body(index)
    else:
        lax.fori_loop(0, count, lambda index, none: (body(index), none)[1], 0)


def start_of(index, size):
    return index * size if isinstance(index, int) else pl.multiple_of(index * size, size)


def partner(me, step, size):
    if size & (size - 1) == 0:
        return me ^ step
    return (me + step) % size


def source(me, step, size):
    if size & (size - 1) == 0:
        return me ^ step
    return (me + size - step) % size


def exchange(value, axis, step):
    size = lax.axis_size(axis)
    return lax.ppermute(value, axis, [(i, partner(i, step, size)) for i in range(size)])


def band_kernel(limit, rows, cols, ids, values, bias, band, bias_out, sums, scaled, here, row, col, sems):
    blocks, tile, _ = sums.shape
    row_blocks = band.shape[1] // tile
    slots = rows.shape[-1]
    ids_here, values_here = here
    lanes = ids_here.shape[0] // slots
    pairs = ((ids, ids_here), (values, values_here), (rows, row), (cols, col), (bias, bias_out))
    copies = [pltpu.make_async_copy(a, b, sems.at[i]) for i, (a, b) in enumerate(pairs)]
    for copy in copies:
        copy.start()

    def clear(index):
        sums[index] = jnp.zeros((tile, tile), f32)

    each(blocks, clear)
    for copy in copies:
        copy.wait()
    line = lax.broadcasted_iota(jnp.int32, scaled.shape, 0)
    scaled[...] = jnp.where(line < limit[0, 0] * lanes, values_here[...].astype(f32), 0.0)
    which = lax.broadcasted_iota(jnp.int32, (tile, tile), 0)

    def add(slot):
        block = col[0, 0, slot] * row_blocks + row[0, 0, slot]
        dense = jnp.zeros((tile, tile), f32)
        for lane in range(lanes):
            place = pl.ds(slot * lanes + lane, 1)
            dense = jnp.where(which == ids_here[place, :], scaled[place, :], dense)
        sums[block] = sums[block] + dense

    several = next(count for count in (4, 2, 1) if slots % count == 0)

    def group(index, none):
        for other in range(several):
            add(index * several + other)
        return none

    lax.fori_loop(0, (limit[0, 0] + several - 1) // several, group, 0)

    def put(index):
        c, r = index // row_blocks, index % row_blocks
        band[pl.ds(start_of(c, tile), tile), pl.ds(start_of(r, tile), tile)] = sums[index].astype(bf16)

    each(blocks, put)


def make_band(limit, rows, cols, ids, values, bias, row_blocks, col_blocks):
    tile = ids.shape[-1]
    lines = ids.shape[-3] * ids.shape[-2]
    ids = ids.reshape(lines, tile)
    values = values.reshape(lines, tile)
    bias = bias.reshape(1, -1)
    out = struct((col_blocks * tile, row_blocks * tile), bf16)
    sums = struct((col_blocks * row_blocks, tile, tile), f32)
    return pl.pallas_call(
        band_kernel,
        out_shape=(out, struct(bias.shape, f32)),
        in_specs=[smem()] + [pl.BlockSpec(memory_space=pltpu.HBM)] * 5,
        out_specs=(vmem(), vmem()),
        scratch_shapes=[
            pltpu.VMEM(sums.shape, f32),
            pltpu.VMEM((lines, tile), f32),
            (pltpu.VMEM((lines, tile), jnp.int32), pltpu.VMEM((lines, tile), bf16)),
            pltpu.SMEM(rows.shape, jnp.int32),
            pltpu.SMEM(cols.shape, jnp.int32),
            pltpu.SemaphoreType.DMA((5,)),
        ],
        compiler_params=pltpu.CompilerParams(vmem_limit_bytes=grant + sums.size * 4 + out.size * 2),
        cost_estimate=pl.CostEstimate(flops=8 * sums.size * 8, bytes_accessed=8 * 2**20, transcendentals=0),
        name="band",
    )(limit, *[pltpu.with_memory_space_constraint(a, pltpu.HBM) for a in (rows, cols, ids, values, bias)])


def forward_kernel(size, owners, *refs):
    parts, (band, out, panel) = refs[:size], refs[size:]
    me = lax.axis_index("row")
    width = parts[0].shape[0]
    for step, part in enumerate(parts):
        slot = pl.multiple_of(source(me, step, size) * width, width)
        panel[pl.ds(slot, width), :] = part[...].astype(f32)
    left = panel[...].astype(bf16)
    own = out.shape[2]
    many = min(wide, band.shape[1])

    def piece(index):
        got = dot(left, band[:, pl.ds(start_of(index, many), many)]).astype(bf16)
        for part in range(many // own):
            out[index * (many // own) + part] = got[:, part * own : (part + 1) * own]

    each(band.shape[1] // many, piece)


def forward(parts, band, owners):
    hidden = parts[0].shape[0] * len(parts)
    nodes, total = band.shape
    return pl.pallas_call(
        functools.partial(forward_kernel, len(parts), owners),
        out_shape=struct((owners, hidden, total // owners), bf16),
        in_specs=[vmem()] * (len(parts) + 1),
        out_specs=vmem(),
        scratch_shapes=[pltpu.VMEM((hidden, nodes), f32)],
        compiler_params=room(band),
        name="forward",
    )(*parts, band)


def pair_rows(line):
    high = line.astype(bf16).astype(f32)
    row = lax.broadcasted_iota(jnp.int32, (tail, line.shape[1]), 0)
    return jnp.where(row == 0, high, jnp.where(row == 1, line - high, 0.0))


def shares_of(size):
    return 2 if size % 2 == 0 else 1


def own_kernel(shares, got, weight, bias, cotangent, act, grad_out, kept, sent, bias_out, part):
    owners, hidden, own = got.shape
    share = hidden // shares
    total = got[0].astype(f32)
    for index in range(1, owners):
        total = total + got[index].astype(f32)
    high = total.astype(bf16)
    low = (total - high.astype(f32)).astype(bf16)
    pre = dot(high, weight[...], 0, 0) + dot(low, weight[...], 0, 0) + bias[...]
    squashed = jax.nn.sigmoid(pre)
    act[...] = pre * squashed
    grad = cotangent[...] * squashed * (1.0 + pre * (1.0 - squashed))
    grad = grad.astype(bf16)
    grad_out[...] = grad
    part[...] = dot(high, grad) + dot(low, grad)
    bias_out[...] = pair_rows(jnp.sum(grad.astype(f32), axis=0, keepdims=True)).astype(bf16)
    mine = lax.rem(lax.axis_index("row"), shares)
    kept[...] = part[pl.ds(pl.multiple_of(mine * share, share), share), :]
    sent[...] = part[pl.ds(pl.multiple_of((shares - 1 - mine) * share, share), share), :].astype(bf16)


def own_rows(got, weight, bias, cotangent, shares):
    owners, hidden, own = got.shape
    share = hidden // shares
    return pl.pallas_call(
        functools.partial(own_kernel, shares),
        out_shape=(
            struct(cotangent.shape, f32),
            struct(cotangent.shape, bf16),
            struct((share, hidden), f32),
            struct((share, hidden), bf16),
            struct((tail, hidden), bf16),
        ),
        in_specs=[vmem()] * 4,
        out_specs=(vmem(),) * 5,
        scratch_shapes=[pltpu.VMEM((hidden, hidden), f32)],
        compiler_params=room(got),
        name="own_rows",
    )(got, weight, bias, cotangent)


def turn_kernel(grad, weight, back):
    back[...] = dot(weight[...], grad[...], 1, 1).astype(bf16)


def turn(grad, weight):
    own, hidden = grad.shape
    return pl.pallas_call(
        turn_kernel,
        out_shape=struct((hidden, own), bf16),
        in_specs=[vmem()] * 2,
        out_specs=vmem(),
        compiler_params=room(grad, weight),
        name="turn",
    )(grad, weight)


def gather_kernel(shares, back, kept, got, bias, message):
    owners, _, own = message.shape
    hidden = back.shape[0]
    share = kept.shape[0]
    total = kept[...]
    if shares > 1:
        total = total + got[...].astype(f32)
    total = total.astype(bf16)
    for index in range(owners):
        message[index, :hidden, :] = back[...]
        message[index, hidden : hidden + share, :] = total
        message[index, hidden + share :, :] = bias[...]


def gather(back, kept, got, bias, shares, owners):
    hidden, own = back.shape
    rows = hidden + kept.shape[0] + bias.shape[0]
    return pl.pallas_call(
        functools.partial(gather_kernel, shares),
        out_shape=struct((owners, rows, own), bf16),
        in_specs=[vmem()] * 4,
        out_specs=vmem(),
        compiler_params=room(back),
        name="gather",
    )(back, kept, got, bias)


def backward_kernel(size, share, got, band, *refs):
    messages, (kept, wide_rows, grads, packed) = refs[:size], refs[size:]
    owners, _, own = got.shape
    width, nodes = kept.shape
    hidden = width * size
    me = lax.axis_index("row")
    weight_part = jnp.zeros((share, own), f32)
    bias_part = jnp.zeros((1, own), f32)
    for index in range(owners):
        wide_rows[:, index * own : (index + 1) * own] = got[index, :hidden, :]
        weight_part = weight_part + got[index, hidden : hidden + share, :].astype(f32)
        bias_part = bias_part + jnp.sum(got[index, hidden + share :, :].astype(f32), axis=0, keepdims=True)
    many = min(wide, nodes)

    def piece(index):
        place = pl.ds(start_of(index, many), many)
        grads[:, place] = dot(wide_rows[...], band[place, :], 1, 1)

    each(nodes // many, piece)
    split = nodes // own
    packed[split * width : split * width + share, :] = weight_part
    packed[split * width + share :, :] = pair_rows(bias_part)
    for step in range(size):
        slot = pl.multiple_of(partner(me, step, size) * width, width)
        block = grads[pl.ds(slot, width), :]
        if step == 0:
            kept[...] = block
        for index in range(split):
            packed[index * width : (index + 1) * width, :] = block[:, index * own : (index + 1) * own]
        messages[step][...] = packed[...].astype(bf16)


def backward(got, band, size, hidden):
    owners, rows, own = got.shape
    nodes, total = band.shape
    width = hidden // size
    share = rows - hidden - tail
    message = struct((width * (nodes // own) + share + tail, own), bf16)
    return pl.pallas_call(
        functools.partial(backward_kernel, size, share),
        out_shape=(message,) * size + (struct((width, nodes), f32),),
        in_specs=[vmem()] * 2,
        out_specs=(vmem(),) * (size + 1),
        scratch_shapes=[
            pltpu.VMEM((hidden, total), bf16),
            pltpu.VMEM((hidden, nodes), f32),
            pltpu.VMEM(message.shape, f32),
        ],
        compiler_params=room(band, got),
        name="backward",
    )(got, band)


def final_kernel(size, shares, shrink, *refs):
    messages, (kept, features, weight, bias, slots) = refs[:size], refs[size:]
    width, nodes = kept.shape
    share = weight.shape[0] // shares
    own = messages[0].shape[1]
    split = nodes // own
    me = lax.axis_index("row")
    for step, message in enumerate(messages):
        slots[source(me, step, size)] = message[split * width :, :].astype(f32)
    for index in range(split):
        place = slice(index * own, (index + 1) * own)
        total = kept[:, place]
        for message in messages[1:]:
            total = total + message[index * width : (index + 1) * width, :].astype(f32)
        features[:, place] = total.astype(bf16)
    bias_part = jnp.zeros((tail, own), f32)
    for half in range(shares):
        total = jnp.zeros((share, own), f32)
        for index in range(half, size, shares):
            total = total + slots[index, :share, :]
            bias_part = bias_part + slots[index, share:, :]
        weight[half * share : (half + 1) * share, :] = total * shrink
    bias[...] = jnp.sum(bias_part, axis=0, keepdims=True) * shrink


def final(messages, kept, hidden, shares, shrink):
    width, nodes = kept.shape
    size = len(messages)
    rows, own = messages[0].shape
    return pl.pallas_call(
        functools.partial(final_kernel, size, shares, shrink),
        out_shape=(struct((width, nodes), bf16), struct((hidden, hidden), f32), struct((1, hidden), f32)),
        in_specs=[vmem()] * (size + 1),
        out_specs=(vmem(),) * 3,
        scratch_shapes=[pltpu.VMEM((size, hidden // shares + tail, own), f32)],
        compiler_params=room(*messages),
        name="final",
    )(*messages, kept)


def shards(
    features,
    weight,
    bias_vector,
    tile_rows,
    tile_cols,
    neighbours,
    edge_weights,
    tile_count,
    cotangent,
):
    tile_size = neighbours.shape[-1]
    hidden = weight.shape[1]
    size, owners = lax.axis_size("row"), lax.axis_size("col")
    blocks_own = cotangent.shape[0] // tile_size
    row_blocks = blocks_own * owners
    col_blocks = blocks_own * size
    turned = features.T
    parts = [turned] + [exchange(turned, "row", step) for step in range(1, size)]
    band, bias = make_band(
        tile_count, tile_rows, tile_cols, neighbours, edge_weights, bias_vector, row_blocks, col_blocks
    )
    sums = forward(parts, band, owners)
    sums = lax.all_to_all(sums, "col", 0, 0, tiled=True)
    shares = shares_of(size)
    activations, grad, kept, sent, bias_part = own_rows(sums, weight, bias, cotangent, shares)
    got = exchange(sent, "row", 1) if shares > 1 else sent
    message = gather(turn(grad, weight), kept, got, bias_part, shares, owners)
    message = lax.all_to_all(message, "col", 0, 0, tiled=True)
    *messages, kept = backward(message, band, size, hidden)
    messages = [messages[0]] + [exchange(messages[step], "row", step) for step in range(1, size)]
    node_count = cotangent.shape[0] * size * owners
    grad_features, grad_weight, grad_bias = final(
        messages, kept, hidden, shares, float(node_count) ** (-0.5)
    )
    return (activations, grad_features.T, grad_weight, grad_bias.reshape(hidden))


def solution(mesh):
    in_specs = (
        P("col", "row"),
        P(),
        P(),
        P("row", "col", None),
        P("row", "col", None),
        P("row", "col", None, None, None),
        P("row", "col", None, None, None),
        P("row", "col"),
        P(("row", "col"), None),
    )
    out_specs = (P(("row", "col"), None), P("col", "row"), P(), P())
    return jax.shard_map(shards, mesh=mesh, in_specs=in_specs, out_specs=out_specs, check_vma=False)
```

```python
import functools

import jax
import jax.numpy as jnp
from jax import lax
from jax.experimental import pallas as pl
from jax.experimental.pallas import tpu as pltpu
from jax.sharding import PartitionSpec as P

f32 = jnp.float32
bf16 = jnp.bfloat16
tail = 16
wide = 1024
grant = 8 * 2**20


def room(*arrays):
    size = sum(a.size * a.dtype.itemsize for a in arrays)
    return pltpu.CompilerParams(vmem_limit_bytes=grant + 2 * size)


def vmem():
    return pl.BlockSpec(memory_space=pltpu.VMEM)


def smem():
    return pl.BlockSpec(memory_space=pltpu.SMEM)


def struct(shape, dtype):
    return jax.ShapeDtypeStruct(shape, dtype)


def dims(left, right):
    return (((left,), (right,)), ((), ()))


def dot(a, b, left=1, right=0):
    return lax.dot_general(a, b, dims(left, right), preferred_element_type=f32)


def each(count, body):
    if count <= 64:
        for index in range(count):
            body(index)
    else:
        lax.fori_loop(0, count, lambda index, none: (body(index), none)[1], 0)


def start_of(index, size):
    return index * size if isinstance(index, int) else pl.multiple_of(index * size, size)


def partner(me, step, size):
    if size & (size - 1) == 0:
        return me ^ step
    return (me + step) % size


def source(me, step, size):
    if size & (size - 1) == 0:
        return me ^ step
    return (me + size - step) % size


def exchange(value, axis, step):
    size = lax.axis_size(axis)
    return lax.ppermute(value, axis, [(i, partner(i, step, size)) for i in range(size)])


def band_kernel(limit, rows, cols, ids, values, bias, band, bias_out, sums, scaled, here, row, col, sems):
    blocks, tile, _ = sums.shape
    row_blocks = band.shape[1] // tile
    slots = rows.shape[-1]
    ids_here, values_here = here
    lanes = ids_here.shape[0] // slots
    pairs = ((ids, ids_here), (values, values_here), (rows, row), (cols, col), (bias, bias_out))
    copies = [pltpu.make_async_copy(a, b, sems.at[i]) for i, (a, b) in enumerate(pairs)]
    for copy in copies:
        copy.start()

    def clear(index):
        sums[index] = jnp.zeros((tile, tile), f32)

    each(blocks, clear)
    for copy in copies:
        copy.wait()
    line = lax.broadcasted_iota(jnp.int32, scaled.shape, 0)
    scaled[...] = jnp.where(line < limit[0, 0] * lanes, values_here[...].astype(f32), 0.0)
    which = lax.broadcasted_iota(jnp.int32, (tile, tile), 0)

    def add(slot):
        block = col[0, 0, slot] * row_blocks + row[0, 0, slot]
        dense = jnp.zeros((tile, tile), f32)
        for lane in range(lanes):
            place = pl.ds(slot * lanes + lane, 1)
            dense = jnp.where(which == ids_here[place, :], scaled[place, :], dense)
        sums[block] = sums[block] + dense

    several = next(count for count in (4, 2, 1) if slots % count == 0)

    def group(index, none):
        for other in range(several):
            add(index * several + other)
        return none

    lax.fori_loop(0, (limit[0, 0] + several - 1) // several, group, 0)

    def put(index):
        c, r = index // row_blocks, index % row_blocks
        band[pl.ds(start_of(c, tile), tile), pl.ds(start_of(r, tile), tile)] = sums[index].astype(bf16)

    each(blocks, put)


def make_band(limit, rows, cols, ids, values, bias, row_blocks, col_blocks):
    tile = ids.shape[-1]
    lines = ids.shape[-3] * ids.shape[-2]
    ids = ids.reshape(lines, tile)
    values = values.reshape(lines, tile)
    bias = bias.reshape(1, -1)
    out = struct((col_blocks * tile, row_blocks * tile), bf16)
    sums = struct((col_blocks * row_blocks, tile, tile), f32)
    return pl.pallas_call(
        band_kernel,
        out_shape=(out, struct(bias.shape, f32)),
        in_specs=[smem()] + [pl.BlockSpec(memory_space=pltpu.HBM)] * 5,
        out_specs=(vmem(), vmem()),
        scratch_shapes=[
            pltpu.VMEM(sums.shape, f32),
            pltpu.VMEM((lines, tile), f32),
            (pltpu.VMEM((lines, tile), jnp.int32), pltpu.VMEM((lines, tile), bf16)),
            pltpu.SMEM(rows.shape, jnp.int32),
            pltpu.SMEM(cols.shape, jnp.int32),
            pltpu.SemaphoreType.DMA((5,)),
        ],
        compiler_params=pltpu.CompilerParams(vmem_limit_bytes=grant + sums.size * 4 + out.size * 2),
        cost_estimate=pl.CostEstimate(flops=8 * sums.size * 8, bytes_accessed=8 * 2**20, transcendentals=0),
        name="band",
    )(limit, *[pltpu.with_memory_space_constraint(a, pltpu.HBM) for a in (rows, cols, ids, values, bias)])


def forward_kernel(size, owners, *refs):
    parts, (band, out, panel) = refs[:size], refs[size:]
    me = lax.axis_index("row")
    width = parts[0].shape[0]
    for step, part in enumerate(parts):
        slot = pl.multiple_of(source(me, step, size) * width, width)
        panel[pl.ds(slot, width), :] = part[...].astype(f32)
    left = panel[...].astype(bf16)
    own = out.shape[2]
    many = min(wide, band.shape[1])

    def piece(index):
        got = dot(left, band[:, pl.ds(start_of(index, many), many)]).astype(bf16)
        for part in range(many // own):
            out[index * (many // own) + part] = got[:, part * own : (part + 1) * own]

    each(band.shape[1] // many, piece)


def forward(parts, band, owners):
    hidden = parts[0].shape[0] * len(parts)
    nodes, total = band.shape
    return pl.pallas_call(
        functools.partial(forward_kernel, len(parts), owners),
        out_shape=struct((owners, hidden, total // owners), bf16),
        in_specs=[vmem()] * (len(parts) + 1),
        out_specs=vmem(),
        scratch_shapes=[pltpu.VMEM((hidden, nodes), f32)],
        compiler_params=room(band),
        name="forward",
    )(*parts, band)


def pair_rows(line):
    high = line.astype(bf16).astype(f32)
    row = lax.broadcasted_iota(jnp.int32, (tail, line.shape[1]), 0)
    return jnp.where(row == 0, high, jnp.where(row == 1, line - high, 0.0))


def shares_of(size):
    return 2 if size % 2 == 0 else 1


def own_kernel(shares, got, weight, bias, cotangent, pre_out, grad_out, kept, sent, part):
    owners, hidden, own = got.shape
    share = hidden // shares
    total = got[0].astype(f32)
    for index in range(1, owners):
        total = total + got[index].astype(f32)
    high = total.astype(bf16)
    low = (total - high.astype(f32)).astype(bf16)
    pre = dot(high, weight[...], 0, 0) + dot(low, weight[...], 0, 0) + bias[...]
    pre_out[...] = pre
    squashed = jax.nn.sigmoid(pre)
    grad = cotangent[...] * squashed * (1.0 + pre * (1.0 - squashed))
    grad = grad.astype(bf16)
    grad_out[...] = grad
    part[...] = dot(high, grad) + dot(low, grad)
    mine = lax.rem(lax.axis_index("row"), shares)
    kept[...] = part[pl.ds(pl.multiple_of(mine * share, share), share), :]
    sent[...] = part[pl.ds(pl.multiple_of((shares - 1 - mine) * share, share), share), :].astype(bf16)


def own_rows(got, weight, bias, cotangent, shares):
    owners, hidden, own = got.shape
    share = hidden // shares
    return pl.pallas_call(
        functools.partial(own_kernel, shares),
        out_shape=(
            struct(cotangent.shape, f32),
            struct(cotangent.shape, bf16),
            struct((share, hidden), f32),
            struct((share, hidden), bf16),
        ),
        in_specs=[vmem()] * 4,
        out_specs=(vmem(),) * 4,
        scratch_shapes=[pltpu.VMEM((hidden, hidden), f32)],
        compiler_params=room(got),
        name="own_rows",
    )(got, weight, bias, cotangent)


def activate_kernel(pre, act):
    act[...] = pre[...] * jax.nn.sigmoid(pre[...])


def activate(pre):
    return pl.pallas_call(
        activate_kernel,
        out_shape=struct(pre.shape, f32),
        in_specs=[vmem()],
        out_specs=vmem(),
        compiler_params=room(pre),
        name="activate",
    )(pre)


def gather_kernel(shares, grad, kept, got, message):
    owners = message.shape[0]
    own = grad.shape[0]
    total = kept[...]
    if shares > 1:
        total = total + got[...].astype(f32)
    total = total.astype(bf16)
    for index in range(owners):
        message[index, :own, :] = grad[...]
        message[index, own:, :] = total


def gather(grad, kept, got, shares, owners):
    own, hidden = grad.shape
    return pl.pallas_call(
        functools.partial(gather_kernel, shares),
        out_shape=struct((owners, own + kept.shape[0], hidden), bf16),
        in_specs=[vmem()] * 3,
        out_specs=vmem(),
        compiler_params=room(grad),
        name="gather",
    )(grad, kept, got)


def backward_kernel(size, own, got, weight, band, *refs):
    messages, (kept, rows, back, grads, packed) = refs[:size], refs[size:]
    owners, lines, hidden = got.shape
    share = lines - own
    width, nodes = kept.shape
    me = lax.axis_index("row")
    weight_part = jnp.zeros((share, hidden), f32)
    for index in range(owners):
        rows[index * own : (index + 1) * own, :] = got[index, :own, :]
        weight_part = weight_part + got[index, own:, :].astype(f32)
    back[...] = dot(weight[...], rows[...], 1, 1).astype(bf16)
    many = min(wide, nodes)

    def piece(index):
        place = pl.ds(start_of(index, many), many)
        grads[:, place] = dot(back[...], band[place, :], 1, 1)

    each(nodes // many, piece)
    split = nodes // hidden
    packed[split * width : split * width + share, :] = weight_part
    packed[split * width + share :, :] = pair_rows(jnp.sum(rows[...].astype(f32), axis=0, keepdims=True))
    for step in range(size):
        slot = pl.multiple_of(partner(me, step, size) * width, width)
        block = grads[pl.ds(slot, width), :]
        if step == 0:
            kept[...] = block
        for index in range(split):
            packed[index * width : (index + 1) * width, :] = block[:, index * hidden : (index + 1) * hidden]
        messages[step][...] = packed[...].astype(bf16)


def backward(got, weight, band, size, own):
    owners, lines, hidden = got.shape
    nodes, total = band.shape
    width = hidden // size
    message = struct((width * (nodes // hidden) + lines - own + tail, hidden), bf16)
    return pl.pallas_call(
        functools.partial(backward_kernel, size, own),
        out_shape=(message,) * size + (struct((width, nodes), f32),),
        in_specs=[vmem()] * 3,
        out_specs=(vmem(),) * (size + 1),
        scratch_shapes=[
            pltpu.VMEM((total, hidden), bf16),
            pltpu.VMEM((hidden, total), bf16),
            pltpu.VMEM((hidden, nodes), f32),
            pltpu.VMEM(message.shape, f32),
        ],
        compiler_params=room(band, got),
        name="backward",
    )(got, weight, band)


def final_kernel(size, shares, shrink, *refs):
    messages, (kept, features, weight, bias, slots) = refs[:size], refs[size:]
    width, nodes = kept.shape
    share = weight.shape[0] // shares
    own = messages[0].shape[1]
    split = nodes // own
    me = lax.axis_index("row")
    for step, message in enumerate(messages):
        slots[source(me, step, size)] = message[split * width :, :].astype(f32)
    for index in range(split):
        place = slice(index * own, (index + 1) * own)
        total = kept[:, place]
        for message in messages[1:]:
            total = total + message[index * width : (index + 1) * width, :].astype(f32)
        features[:, place] = total.astype(bf16)
    bias_part = jnp.zeros((tail, own), f32)
    for half in range(shares):
        total = jnp.zeros((share, own), f32)
        for index in range(half, size, shares):
            total = total + slots[index, :share, :]
            bias_part = bias_part + slots[index, share:, :]
        weight[half * share : (half + 1) * share, :] = total * shrink
    bias[...] = jnp.sum(bias_part, axis=0, keepdims=True) * shrink


def final(messages, kept, hidden, shares, shrink):
    width, nodes = kept.shape
    size = len(messages)
    rows, own = messages[0].shape
    return pl.pallas_call(
        functools.partial(final_kernel, size, shares, shrink),
        out_shape=(struct((width, nodes), bf16), struct((hidden, hidden), f32), struct((1, hidden), f32)),
        in_specs=[vmem()] * (size + 1),
        out_specs=(vmem(),) * 3,
        scratch_shapes=[pltpu.VMEM((size, hidden // shares + tail, own), f32)],
        compiler_params=room(*messages),
        name="final",
    )(*messages, kept)


def shards(
    features,
    weight,
    bias_vector,
    tile_rows,
    tile_cols,
    neighbours,
    edge_weights,
    tile_count,
    cotangent,
):
    tile_size = neighbours.shape[-1]
    hidden = weight.shape[1]
    size, owners = lax.axis_size("row"), lax.axis_size("col")
    blocks_own = cotangent.shape[0] // tile_size
    row_blocks = blocks_own * owners
    col_blocks = blocks_own * size
    turned = features.T
    parts = [turned] + [exchange(turned, "row", step) for step in range(1, size)]
    band, bias = make_band(
        tile_count, tile_rows, tile_cols, neighbours, edge_weights, bias_vector, row_blocks, col_blocks
    )
    sums = forward(parts, band, owners)
    sums = lax.all_to_all(sums, "col", 0, 0, tiled=True)
    shares = shares_of(size)
    pre, grad, kept, sent = own_rows(sums, weight, bias, cotangent, shares)
    got = exchange(sent, "row", 1) if shares > 1 else sent
    activations = activate(pre)
    message = gather(grad, kept, got, shares, owners)
    message = lax.all_to_all(message, "col", 0, 0, tiled=True)
    *messages, kept = backward(message, weight, band, size, cotangent.shape[0])
    messages = [messages[0]] + [exchange(messages[step], "row", step) for step in range(1, size)]
    node_count = cotangent.shape[0] * size * owners
    grad_features, grad_weight, grad_bias = final(
        messages, kept, hidden, shares, float(node_count) ** (-0.5)
    )
    return (activations, grad_features.T, grad_weight, grad_bias.reshape(hidden))


def solution(mesh):
    in_specs = (
        P("col", "row"),
        P(),
        P(),
        P("row", "col", None),
        P("row", "col", None),
        P("row", "col", None, None, None),
        P("row", "col", None, None, None),
        P("row", "col"),
        P(("row", "col"), None),
    )
    out_specs = (P(("row", "col"), None), P("col", "row"), P(), P())
    return jax.shard_map(shards, mesh=mesh, in_specs=in_specs, out_specs=out_specs, check_vma=False)
```

```python
import functools

import jax
import jax.numpy as jnp
from jax import lax
from jax.experimental import pallas as pl
from jax.experimental.pallas import tpu as pltpu
from jax.sharding import PartitionSpec as P

f32 = jnp.float32
bf16 = jnp.bfloat16
tail = 16
wide = 1024
grant = 8 * 2**20


def room(*arrays):
    size = sum(a.size * a.dtype.itemsize for a in arrays)
    return pltpu.CompilerParams(vmem_limit_bytes=grant + 2 * size)


def vmem():
    return pl.BlockSpec(memory_space=pltpu.VMEM)


def smem():
    return pl.BlockSpec(memory_space=pltpu.SMEM)


def struct(shape, dtype):
    return jax.ShapeDtypeStruct(shape, dtype)


def dims(left, right):
    return (((left,), (right,)), ((), ()))


def dot(a, b, left=1, right=0):
    return lax.dot_general(a, b, dims(left, right), preferred_element_type=f32)


def each(count, body):
    if count <= 64:
        for index in range(count):
            body(index)
    else:
        lax.fori_loop(0, count, lambda index, none: (body(index), none)[1], 0)


def start_of(index, size):
    return index * size if isinstance(index, int) else pl.multiple_of(index * size, size)


def partner(me, step, size):
    if size & (size - 1) == 0:
        return me ^ step
    return (me + step) % size


def source(me, step, size):
    if size & (size - 1) == 0:
        return me ^ step
    return (me + size - step) % size


def exchange(value, axis, step, near=1):
    far = lax.axis_size(axis) // near
    pairs = [(i * near + j, partner(i, step, far) * near + j) for i in range(far) for j in range(near)]
    return lax.ppermute(value, axis, pairs)


def exchange_near(value, axis, near):
    size = lax.axis_size(axis)
    return lax.ppermute(value, axis, [(i, i // near * near + (near - 1 - i % near)) for i in range(size)])


def band_kernel(limit, rows, cols, ids, values, bias, band, bias_out, sums, scaled, here, row, col, sems):
    blocks, tile, _ = sums.shape
    row_blocks = band.shape[1] // tile
    slots = rows.shape[-1]
    ids_here, values_here = here
    lanes = ids_here.shape[0] // slots
    pairs = ((ids, ids_here), (values, values_here), (rows, row), (cols, col), (bias, bias_out))
    copies = [pltpu.make_async_copy(a, b, sems.at[i]) for i, (a, b) in enumerate(pairs)]
    for copy in copies:
        copy.start()

    def clear(index):
        sums[index] = jnp.zeros((tile, tile), f32)

    each(blocks, clear)
    for copy in copies:
        copy.wait()
    line = lax.broadcasted_iota(jnp.int32, scaled.shape, 0)
    scaled[...] = jnp.where(line < limit[0, 0] * lanes, values_here[...].astype(f32), 0.0)
    which = lax.broadcasted_iota(jnp.int32, (tile, tile), 0)

    def add(slot):
        block = col[0, 0, slot] * row_blocks + row[0, 0, slot]
        dense = jnp.zeros((tile, tile), f32)
        for lane in range(lanes):
            place = pl.ds(slot * lanes + lane, 1)
            dense = jnp.where(which == ids_here[place, :], scaled[place, :], dense)
        sums[block] = sums[block] + dense

    several = next(count for count in (4, 2, 1) if slots % count == 0)

    def group(index, none):
        for other in range(several):
            add(index * several + other)
        return none

    lax.fori_loop(0, (limit[0, 0] + several - 1) // several, group, 0)

    def put(index):
        c, r = index // row_blocks, index % row_blocks
        band[pl.ds(start_of(c, tile), tile), pl.ds(start_of(r, tile), tile)] = sums[index].astype(bf16)

    each(blocks, put)


def make_band(limit, rows, cols, ids, values, bias, row_blocks, col_blocks):
    tile = ids.shape[-1]
    lines = ids.shape[-3] * ids.shape[-2]
    ids = ids.reshape(lines, tile)
    values = values.reshape(lines, tile)
    bias = bias.reshape(1, -1)
    out = struct((col_blocks * tile, row_blocks * tile), bf16)
    sums = struct((col_blocks * row_blocks, tile, tile), f32)
    return pl.pallas_call(
        band_kernel,
        out_shape=(out, struct(bias.shape, f32)),
        in_specs=[smem()] + [pl.BlockSpec(memory_space=pltpu.HBM)] * 5,
        out_specs=(vmem(), vmem()),
        scratch_shapes=[
            pltpu.VMEM(sums.shape, f32),
            pltpu.VMEM((lines, tile), f32),
            (pltpu.VMEM((lines, tile), jnp.int32), pltpu.VMEM((lines, tile), bf16)),
            pltpu.SMEM(rows.shape, jnp.int32),
            pltpu.SMEM(cols.shape, jnp.int32),
            pltpu.SemaphoreType.DMA((5,)),
        ],
        compiler_params=pltpu.CompilerParams(vmem_limit_bytes=grant + sums.size * 4 + out.size * 2),
        cost_estimate=pl.CostEstimate(flops=8 * sums.size * 8, bytes_accessed=8 * 2**20, transcendentals=0),
        name="band",
    )(limit, *[pltpu.with_memory_space_constraint(a, pltpu.HBM) for a in (rows, cols, ids, values, bias)])


def forward_kernel(size, near, *refs):
    parts, (band, kept), messages, (panel, sums) = refs[:size], refs[size : size + 2], refs[size + 2 : -2], refs[-2:]
    me = lax.axis_index("row")
    mine = lax.axis_index("col") // near
    far, _, own = sums.shape
    width = parts[0].shape[0]
    for step, part in enumerate(parts):
        slot = pl.multiple_of(source(me, step, size) * width, width)
        panel[pl.ds(slot, width), :] = part[...].astype(f32)
    left = panel[...].astype(bf16)
    many = max(own, min(wide, band.shape[1]))

    def piece(index):
        got = dot(left, band[:, pl.ds(start_of(index, many), many)])
        for part in range(many // own):
            sums[index * (many // own) + part] = got[:, part * own : (part + 1) * own]

    each(band.shape[1] // many, piece)
    kept[...] = sums[mine]
    for step, message in enumerate(messages):
        message[...] = sums[partner(mine, step + 1, far)].astype(bf16)


def forward(parts, band, far, near):
    hidden = parts[0].shape[0] * len(parts)
    nodes, total = band.shape
    block = (hidden, total // far)
    return pl.pallas_call(
        functools.partial(forward_kernel, len(parts), near),
        out_shape=(struct(block, f32),) + (struct(block, bf16),) * (far - 1),
        in_specs=[vmem()] * (len(parts) + 1),
        out_specs=(vmem(),) * far,
        scratch_shapes=[pltpu.VMEM((hidden, nodes), f32), pltpu.VMEM((far,) + block, f32)],
        compiler_params=room(band, struct((far,) + block, f32)),
        name="forward",
    )(*parts, band)


def add_kernel(kept, *refs):
    parts, out = refs[:-1], refs[-1]
    total = kept[...]
    for part in parts:
        total = total + part[...].astype(f32)
    out[...] = total.astype(bf16)


def add(kept, parts):
    return pl.pallas_call(
        add_kernel,
        out_shape=struct(kept.shape, bf16),
        in_specs=[vmem()] * (len(parts) + 1),
        out_specs=vmem(),
        compiler_params=room(kept),
        name="add",
    )(kept, *parts)


def pair_rows(line):
    high = line.astype(bf16).astype(f32)
    row = lax.broadcasted_iota(jnp.int32, (tail, line.shape[1]), 0)
    return jnp.where(row == 0, high, jnp.where(row == 1, line - high, 0.0))


def own_kernel(near, *refs):
    sums, (weight, bias), cotangents = refs[:near], refs[near : near + 2], refs[near + 2 : 2 * near + 2]
    pre_out, message, wide_pre, given = refs[2 * near + 2 :]
    mine = lax.rem(lax.axis_index("col"), near)
    own = cotangents[0].shape[0]
    total = sums[0][...].astype(f32)
    for part in sums[1:]:
        total = total + part[...].astype(f32)
    for index, part in enumerate(cotangents):
        place = mine if index == 0 else near - 1 - mine
        given[pl.ds(pl.multiple_of(place * own, own), own), :] = part[...]
    high = total.astype(bf16)
    low = (total - high.astype(f32)).astype(bf16)
    pre = dot(high, weight[...], 0, 0) + dot(low, weight[...], 0, 0) + bias[...]
    wide_pre[...] = pre
    squashed = jax.nn.sigmoid(pre)
    grad = given[...] * squashed * (1.0 + pre * (1.0 - squashed))
    grad = grad.astype(bf16)
    rows = grad.shape[0]
    message[:rows, :] = grad
    message[rows:, :] = (dot(high, grad) + dot(low, grad)).astype(bf16)
    pre_out[...] = wide_pre[pl.ds(pl.multiple_of(mine * own, own), own), :]


def own_rows(sums, weight, bias, cotangents):
    near = len(sums)
    hidden, rows = sums[0].shape
    own = cotangents[0].shape[0]
    return pl.pallas_call(
        functools.partial(own_kernel, near),
        out_shape=(struct((own, hidden), f32), struct((rows + hidden, hidden), bf16)),
        in_specs=[vmem()] * (2 * near + 2),
        out_specs=(vmem(),) * 2,
        scratch_shapes=[pltpu.VMEM((rows, hidden), f32), pltpu.VMEM((rows, hidden), f32)],
        compiler_params=room(*sums),
        name="own_rows",
    )(*sums, weight, bias, *cotangents)


def activate_kernel(pre, act):
    act[...] = pre[...] * jax.nn.sigmoid(pre[...])


def activate(pre):
    return pl.pallas_call(
        activate_kernel,
        out_shape=struct(pre.shape, f32),
        in_specs=[vmem()],
        out_specs=vmem(),
        compiler_params=room(pre),
        name="activate",
    )(pre)


def backward_kernel(size, far, near, *refs):
    got, (weight, band), messages = refs[:far], refs[far : far + 2], refs[far + 2 : far + 2 + size]
    kept, rows, slots, back, grads, packed = refs[far + 2 + size :]
    hidden = weight.shape[0]
    own = got[0].shape[0] - hidden
    width, nodes = kept.shape
    me = lax.axis_index("row")
    mine = lax.axis_index("col") // near
    for step, part in enumerate(got):
        place = source(mine, step, far)
        rows[pl.ds(pl.multiple_of(place * own, own), own), :] = part[:own, :]
        slots[place] = part[own:, :].astype(f32)
    weight_part = slots[0]
    for index in range(1, far):
        weight_part = weight_part + slots[index]
    back[...] = dot(weight[...], rows[...], 1, 1).astype(bf16)
    many = min(wide, nodes)

    def piece(index):
        place = pl.ds(start_of(index, many), many)
        grads[:, place] = dot(back[...], band[place, :], 1, 1)

    each(nodes // many, piece)
    split = nodes // hidden
    packed[split * width : split * width + hidden, :] = weight_part
    packed[split * width + hidden :, :] = pair_rows(jnp.sum(rows[...].astype(f32), axis=0, keepdims=True))
    for step in range(size):
        slot = pl.multiple_of(partner(me, step, size) * width, width)
        block = grads[pl.ds(slot, width), :]
        if step == 0:
            kept[...] = block
        for index in range(split):
            packed[index * width : (index + 1) * width, :] = block[:, index * hidden : (index + 1) * hidden]
        messages[step][...] = packed[...].astype(bf16)


def backward(got, weight, band, size, near):
    far = len(got)
    hidden = weight.shape[0]
    nodes, total = band.shape
    width = hidden // size
    message = struct((width * (nodes // hidden) + hidden + tail, hidden), bf16)
    return pl.pallas_call(
        functools.partial(backward_kernel, size, far, near),
        out_shape=(message,) * size + (struct((width, nodes), f32),),
        in_specs=[vmem()] * (far + 2),
        out_specs=(vmem(),) * (size + 1),
        scratch_shapes=[
            pltpu.VMEM((total, hidden), bf16),
            pltpu.VMEM((far, hidden, hidden), f32),
            pltpu.VMEM((hidden, total), bf16),
            pltpu.VMEM((hidden, nodes), f32),
            pltpu.VMEM(message.shape, f32),
        ],
        compiler_params=room(band, *got),
        name="backward",
    )(*got, weight, band)


def final_kernel(size, shrink, *refs):
    messages, (kept, features, weight, bias, slots) = refs[:size], refs[size:]
    width, nodes = kept.shape
    hidden = weight.shape[0]
    split = nodes // hidden
    me = lax.axis_index("row")
    for step, message in enumerate(messages):
        slots[source(me, step, size)] = message[split * width :, :].astype(f32)
    for index in range(split):
        place = slice(index * hidden, (index + 1) * hidden)
        total = kept[:, place]
        for message in messages[1:]:
            total = total + message[index * width : (index + 1) * width, :].astype(f32)
        features[:, place] = total.astype(bf16)
    total = slots[0]
    for index in range(1, size):
        total = total + slots[index]
    weight[...] = total[:hidden] * shrink
    bias[...] = jnp.sum(total[hidden:], axis=0, keepdims=True) * shrink


def final(messages, kept, hidden, shrink):
    width, nodes = kept.shape
    size = len(messages)
    return pl.pallas_call(
        functools.partial(final_kernel, size, shrink),
        out_shape=(struct((width, nodes), bf16), struct((hidden, hidden), f32), struct((1, hidden), f32)),
        in_specs=[vmem()] * (size + 1),
        out_specs=(vmem(),) * 3,
        scratch_shapes=[pltpu.VMEM((size, hidden + tail, hidden), f32)],
        compiler_params=room(*messages),
        name="final",
    )(*messages, kept)


def shards(
    features,
    weight,
    bias_vector,
    tile_rows,
    tile_cols,
    neighbours,
    edge_weights,
    tile_count,
    cotangent,
):
    tile_size = neighbours.shape[-1]
    hidden = weight.shape[1]
    size, owners = lax.axis_size("row"), lax.axis_size("col")
    near = 2 if owners % 2 == 0 else 1
    far = owners // near
    blocks_own = cotangent.shape[0] // tile_size
    row_blocks = blocks_own * owners
    col_blocks = blocks_own * size
    turned = features.T
    parts = [turned] + [exchange(turned, "row", step) for step in range(1, size)]
    band, bias = make_band(
        tile_count, tile_rows, tile_cols, neighbours, edge_weights, bias_vector, row_blocks, col_blocks
    )
    kept, *messages = forward(parts, band, far, near)
    got = [exchange(message, "col", step + 1, near) for step, message in enumerate(messages)]
    cotangents = [cotangent]
    if near > 1:
        other, messages[0] = lax.optimization_barrier((cotangent, messages[0]))
        cotangents.append(exchange_near(other, "col", near))
    sums = [add(kept, got)]
    if near > 1:
        sums.append(exchange_near(sums[0], "col", near))
    pre, message = own_rows(sums, weight, bias, cotangents)
    activations = activate(pre)
    got = [message] + [exchange(message, "col", step, near) for step in range(1, far)]
    *messages, kept = backward(got, weight, band, size, near)
    messages = [messages[0]] + [exchange(messages[step], "row", step) for step in range(1, size)]
    node_count = cotangent.shape[0] * size * owners
    grad_features, grad_weight, grad_bias = final(messages, kept, hidden, float(node_count) ** (-0.5))
    return (activations, grad_features.T, grad_weight, grad_bias.reshape(hidden))


def solution(mesh):
    in_specs = (
        P("col", "row"),
        P(),
        P(),
        P("row", "col", None),
        P("row", "col", None),
        P("row", "col", None, None, None),
        P("row", "col", None, None, None),
        P("row", "col"),
        P(("row", "col"), None),
    )
    out_specs = (P(("row", "col"), None), P("col", "row"), P(), P())
    return jax.shard_map(shards, mesh=mesh, in_specs=in_specs, out_specs=out_specs, check_vma=False)
```

```python
import functools

import jax
import jax.numpy as jnp
from jax import lax
from jax.experimental import pallas as pl
from jax.experimental.pallas import tpu as pltpu
from jax.sharding import PartitionSpec as P

f32 = jnp.float32
bf16 = jnp.bfloat16
tail = 16
wide = 1024
grant = 8 * 2**20


def room(*arrays):
    size = sum(a.size * a.dtype.itemsize for a in arrays)
    return pltpu.CompilerParams(vmem_limit_bytes=grant + 2 * size)


def vmem():
    return pl.BlockSpec(memory_space=pltpu.VMEM)


def smem():
    return pl.BlockSpec(memory_space=pltpu.SMEM)


def struct(shape, dtype):
    return jax.ShapeDtypeStruct(shape, dtype)


def dims(left, right):
    return (((left,), (right,)), ((), ()))


def dot(a, b, left=1, right=0):
    return lax.dot_general(a, b, dims(left, right), preferred_element_type=f32)


def each(count, body):
    if count <= 64:
        for index in range(count):
            body(index)
    else:
        lax.fori_loop(0, count, lambda index, none: (body(index), none)[1], 0)


def start_of(index, size):
    return index * size if isinstance(index, int) else pl.multiple_of(index * size, size)


def partner(me, step, size):
    if size & (size - 1) == 0:
        return me ^ step
    return (me + step) % size


def source(me, step, size):
    if size & (size - 1) == 0:
        return me ^ step
    return (me + size - step) % size


def exchange(value, axis, step, members):
    size = lax.axis_size(axis)
    pairs = [(i, i // members * members + partner(i % members, step, members)) for i in range(size)]
    return lax.ppermute(value, axis, pairs)


def exchange_twin(value, axis, members):
    size = lax.axis_size(axis)
    return lax.ppermute(value, axis, [(i, (i + members) % size) for i in range(size)])


def band_kernel(limit, rows, cols, ids, values, bias, band, bias_out, sums, scaled, here, row, col, sems):
    blocks, tile, _ = sums.shape
    row_blocks = band.shape[1] // tile
    slots = rows.shape[-1]
    ids_here, values_here = here
    lanes = ids_here.shape[0] // slots
    pairs = ((ids, ids_here), (values, values_here), (rows, row), (cols, col), (bias, bias_out))
    copies = [pltpu.make_async_copy(a, b, sems.at[i]) for i, (a, b) in enumerate(pairs)]
    for copy in copies:
        copy.start()

    def clear(index):
        sums[index] = jnp.zeros((tile, tile), f32)

    each(blocks, clear)
    for copy in copies:
        copy.wait()
    line = lax.broadcasted_iota(jnp.int32, scaled.shape, 0)
    scaled[...] = jnp.where(line < limit[0, 0] * lanes, values_here[...].astype(f32), 0.0)
    which = lax.broadcasted_iota(jnp.int32, (tile, tile), 0)

    def add(slot):
        block = col[0, 0, slot] * row_blocks + row[0, 0, slot]
        dense = jnp.zeros((tile, tile), f32)
        for lane in range(lanes):
            place = pl.ds(slot * lanes + lane, 1)
            dense = jnp.where(which == ids_here[place, :], scaled[place, :], dense)
        sums[block] = sums[block] + dense

    several = next(count for count in (4, 2, 1) if slots % count == 0)

    def group(index, none):
        for other in range(several):
            add(index * several + other)
        return none

    lax.fori_loop(0, (limit[0, 0] + several - 1) // several, group, 0)

    def put(index):
        c, r = index // row_blocks, index % row_blocks
        band[pl.ds(start_of(c, tile), tile), pl.ds(start_of(r, tile), tile)] = sums[index].astype(bf16)

    each(blocks, put)


def make_band(limit, rows, cols, ids, values, bias, row_blocks, col_blocks):
    tile = ids.shape[-1]
    lines = ids.shape[-3] * ids.shape[-2]
    ids = ids.reshape(lines, tile)
    values = values.reshape(lines, tile)
    bias = bias.reshape(1, -1)
    out = struct((col_blocks * tile, row_blocks * tile), bf16)
    sums = struct((col_blocks * row_blocks, tile, tile), f32)
    return pl.pallas_call(
        band_kernel,
        out_shape=(out, struct(bias.shape, f32)),
        in_specs=[smem()] + [pl.BlockSpec(memory_space=pltpu.HBM)] * 5,
        out_specs=(vmem(), vmem()),
        scratch_shapes=[
            pltpu.VMEM(sums.shape, f32),
            pltpu.VMEM((lines, tile), f32),
            (pltpu.VMEM((lines, tile), jnp.int32), pltpu.VMEM((lines, tile), bf16)),
            pltpu.SMEM(rows.shape, jnp.int32),
            pltpu.SMEM(cols.shape, jnp.int32),
            pltpu.SemaphoreType.DMA((5,)),
        ],
        compiler_params=pltpu.CompilerParams(vmem_limit_bytes=grant + sums.size * 4 + out.size * 2),
        cost_estimate=pl.CostEstimate(flops=8 * sums.size * 8, bytes_accessed=8 * 2**20, transcendentals=0),
        name="band",
    )(limit, *[pltpu.with_memory_space_constraint(a, pltpu.HBM) for a in (rows, cols, ids, values, bias)])


def forward_kernel(size, members, *refs):
    parts, (band, kept), messages, (panel, sums) = refs[:size], refs[size : size + 2], refs[size + 2 : -2], refs[-2:]
    me = lax.axis_index("row")
    mine = lax.rem(lax.axis_index("col"), members)
    owners, _, own = sums.shape
    width = parts[0].shape[0]
    for step, part in enumerate(parts):
        slot = pl.multiple_of(source(me, step, size) * width, width)
        panel[pl.ds(slot, width), :] = part[...].astype(f32)
    left = panel[...].astype(bf16)
    many = max(own, min(wide, band.shape[1]))

    def piece(index):
        got = dot(left, band[:, pl.ds(start_of(index, many), many)])
        for part in range(many // own):
            sums[index * (many // own) + part] = got[:, part * own : (part + 1) * own]

    each(band.shape[1] // many, piece)
    for step, message in enumerate((kept,) + messages):
        place = partner(mine, step, members)
        for twin in range(owners // members):
            message[:, twin * own : (twin + 1) * own] = sums[place + twin * members].astype(message.dtype)


def forward(parts, band, owners, members):
    hidden = parts[0].shape[0] * len(parts)
    nodes, total = band.shape
    block = (hidden, total // members)
    sums = struct((owners, hidden, total // owners), f32)
    return pl.pallas_call(
        functools.partial(forward_kernel, len(parts), members),
        out_shape=(struct(block, f32),) + (struct(block, bf16),) * (members - 1),
        in_specs=[vmem()] * (len(parts) + 1),
        out_specs=(vmem(),) * members,
        scratch_shapes=[pltpu.VMEM((hidden, nodes), f32), pltpu.VMEM(sums.shape, f32)],
        compiler_params=room(band, sums),
        name="forward",
    )(*parts, band)


def add_kernel(kept, *refs):
    parts, out = refs[:-1], refs[-1]
    total = kept[...]
    for part in parts:
        total = total + part[...].astype(f32)
    out[...] = total.astype(bf16)


def add(kept, parts):
    return pl.pallas_call(
        add_kernel,
        out_shape=struct(kept.shape, bf16),
        in_specs=[vmem()] * (len(parts) + 1),
        out_specs=vmem(),
        compiler_params=room(kept),
        name="add",
    )(kept, *parts)


def pair_rows(line):
    high = line.astype(bf16).astype(f32)
    row = lax.broadcasted_iota(jnp.int32, (tail, line.shape[1]), 0)
    return jnp.where(row == 0, high, jnp.where(row == 1, line - high, 0.0))


def own_kernel(members, twins, *refs):
    sums, (weight, bias), cotangents = refs[:twins], refs[twins : twins + 2], refs[twins + 2 : 2 * twins + 2]
    pre_out, message, wide_pre, given = refs[2 * twins + 2 :]
    mine = lax.axis_index("col") // members
    own = cotangents[0].shape[0]
    total = sums[0][...].astype(f32)
    for part in sums[1:]:
        total = total + part[...].astype(f32)
    for index, part in enumerate(cotangents):
        place = mine if index == 0 else twins - 1 - mine
        given[pl.ds(pl.multiple_of(place * own, own), own), :] = part[...]
    high = total.astype(bf16)
    low = (total - high.astype(f32)).astype(bf16)
    pre = dot(high, weight[...], 0, 0) + dot(low, weight[...], 0, 0) + bias[...]
    wide_pre[...] = pre
    squashed = jax.nn.sigmoid(pre)
    grad = given[...] * squashed * (1.0 + pre * (1.0 - squashed))
    grad = grad.astype(bf16)
    rows = grad.shape[0]
    message[:rows, :] = grad
    message[rows:, :] = (dot(high, grad) + dot(low, grad)).astype(bf16)
    pre_out[...] = wide_pre[pl.ds(pl.multiple_of(mine * own, own), own), :]


def own_rows(sums, weight, bias, cotangents, members):
    twins = len(sums)
    hidden, rows = sums[0].shape
    own = cotangents[0].shape[0]
    return pl.pallas_call(
        functools.partial(own_kernel, members, twins),
        out_shape=(struct((own, hidden), f32), struct((rows + hidden, hidden), bf16)),
        in_specs=[vmem()] * (2 * twins + 2),
        out_specs=(vmem(),) * 2,
        scratch_shapes=[pltpu.VMEM((rows, hidden), f32), pltpu.VMEM((rows, hidden), f32)],
        compiler_params=room(*sums),
        name="own_rows",
    )(*sums, weight, bias, *cotangents)


def activate_kernel(pre, act):
    act[...] = pre[...] * jax.nn.sigmoid(pre[...])


def activate(pre):
    return pl.pallas_call(
        activate_kernel,
        out_shape=struct(pre.shape, f32),
        in_specs=[vmem()],
        out_specs=vmem(),
        compiler_params=room(pre),
        name="activate",
    )(pre)


def backward_kernel(size, members, twins, *refs):
    got, (weight, band), messages = refs[:members], refs[members : members + 2], refs[members + 2 : members + 2 + size]
    kept, rows, slots, back, grads, packed = refs[members + 2 + size :]
    hidden = weight.shape[0]
    own = rows.shape[0] // (members * twins)
    width, nodes = kept.shape
    me = lax.axis_index("row")
    mine = lax.rem(lax.axis_index("col"), members)
    for step, part in enumerate(got):
        place = source(mine, step, members)
        for twin in range(twins):
            spot = pl.multiple_of((place + twin * members) * own, own)
            rows[pl.ds(spot, own), :] = part[twin * own : (twin + 1) * own, :]
        slots[place] = part[twins * own :, :].astype(f32)
    weight_part = slots[0]
    for index in range(1, members):
        weight_part = weight_part + slots[index]
    back[...] = dot(weight[...], rows[...], 1, 1).astype(bf16)
    many = min(wide, nodes)

    def piece(index):
        place = pl.ds(start_of(index, many), many)
        grads[:, place] = dot(back[...], band[place, :], 1, 1)

    each(nodes // many, piece)
    split = nodes // hidden
    packed[split * width : split * width + hidden, :] = weight_part
    packed[split * width + hidden :, :] = pair_rows(jnp.sum(rows[...].astype(f32), axis=0, keepdims=True))
    for step in range(size):
        slot = pl.multiple_of(partner(me, step, size) * width, width)
        block = grads[pl.ds(slot, width), :]
        if step == 0:
            kept[...] = block
        for index in range(split):
            packed[index * width : (index + 1) * width, :] = block[:, index * hidden : (index + 1) * hidden]
        messages[step][...] = packed[...].astype(bf16)


def backward(got, weight, band, size, twins):
    members = len(got)
    hidden = weight.shape[0]
    nodes, total = band.shape
    width = hidden // size
    message = struct((width * (nodes // hidden) + hidden + tail, hidden), bf16)
    return pl.pallas_call(
        functools.partial(backward_kernel, size, members, twins),
        out_shape=(message,) * size + (struct((width, nodes), f32),),
        in_specs=[vmem()] * (members + 2),
        out_specs=(vmem(),) * (size + 1),
        scratch_shapes=[
            pltpu.VMEM((total, hidden), bf16),
            pltpu.VMEM((members, hidden, hidden), f32),
            pltpu.VMEM((hidden, total), bf16),
            pltpu.VMEM((hidden, nodes), f32),
            pltpu.VMEM(message.shape, f32),
        ],
        compiler_params=room(band, *got),
        name="backward",
    )(*got, weight, band)


def final_kernel(size, shrink, *refs):
    messages, (kept, features, weight, bias, slots) = refs[:size], refs[size:]
    width, nodes = kept.shape
    hidden = weight.shape[0]
    split = nodes // hidden
    me = lax.axis_index("row")
    for step, message in enumerate(messages):
        slots[source(me, step, size)] = message[split * width :, :].astype(f32)
    for index in range(split):
        place = slice(index * hidden, (index + 1) * hidden)
        total = kept[:, place]
        for message in messages[1:]:
            total = total + message[index * width : (index + 1) * width, :].astype(f32)
        features[:, place] = total.astype(bf16)
    total = slots[0]
    for index in range(1, size):
        total = total + slots[index]
    weight[...] = total[:hidden] * shrink
    bias[...] = jnp.sum(total[hidden:], axis=0, keepdims=True) * shrink


def final(messages, kept, hidden, shrink):
    width, nodes = kept.shape
    size = len(messages)
    return pl.pallas_call(
        functools.partial(final_kernel, size, shrink),
        out_shape=(struct((width, nodes), bf16), struct((hidden, hidden), f32), struct((1, hidden), f32)),
        in_specs=[vmem()] * (size + 1),
        out_specs=(vmem(),) * 3,
        scratch_shapes=[pltpu.VMEM((size, hidden + tail, hidden), f32)],
        compiler_params=room(*messages),
        name="final",
    )(*messages, kept)


def shards(
    features,
    weight,
    bias_vector,
    tile_rows,
    tile_cols,
    neighbours,
    edge_weights,
    tile_count,
    cotangent,
):
    tile_size = neighbours.shape[-1]
    hidden = weight.shape[1]
    size, owners = lax.axis_size("row"), lax.axis_size("col")
    twins = 2 if owners % 2 == 0 else 1
    members = owners // twins
    blocks_own = cotangent.shape[0] // tile_size
    row_blocks = blocks_own * owners
    col_blocks = blocks_own * size
    turned = features.T
    parts = [turned] + [exchange(turned, "row", step, size) for step in range(1, size)]
    band, bias = make_band(
        tile_count, tile_rows, tile_cols, neighbours, edge_weights, bias_vector, row_blocks, col_blocks
    )
    kept, *messages = forward(parts, band, owners, members)
    got = [exchange(message, "col", step + 1, members) for step, message in enumerate(messages)]
    cotangents = [cotangent]
    if twins > 1:
        other, messages[0] = lax.optimization_barrier((cotangent, messages[0]))
        cotangents.append(exchange_twin(other, "col", members))
    sums = [add(kept, got)]
    if twins > 1:
        sums.append(exchange_twin(sums[0], "col", members))
    pre, message = own_rows(sums, weight, bias, cotangents, members)
    activations = activate(pre)
    got = [message] + [exchange(message, "col", step, members) for step in range(1, members)]
    *messages, kept = backward(got, weight, band, size, twins)
    messages = [messages[0]] + [exchange(messages[step], "row", step, size) for step in range(1, size)]
    node_count = cotangent.shape[0] * size * owners
    grad_features, grad_weight, grad_bias = final(messages, kept, hidden, float(node_count) ** (-0.5))
    return (activations, grad_features.T, grad_weight, grad_bias.reshape(hidden))


def solution(mesh):
    in_specs = (
        P("col", "row"),
        P(),
        P(),
        P("row", "col", None),
        P("row", "col", None),
        P("row", "col", None, None, None),
        P("row", "col", None, None, None),
        P("row", "col"),
        P(("row", "col"), None),
    )
    out_specs = (P(("row", "col"), None), P("col", "row"), P(), P())
    return jax.shard_map(shards, mesh=mesh, in_specs=in_specs, out_specs=out_specs, check_vma=False)
```

```python
import functools

import jax
import jax.numpy as jnp
from jax import lax
from jax.experimental import pallas as pl
from jax.experimental.pallas import tpu as pltpu
from jax.sharding import PartitionSpec as P

f32 = jnp.float32
bf16 = jnp.bfloat16
tail = 16
wide = 1024
grant = 8 * 2**20


def room(*arrays):
    size = sum(a.size * a.dtype.itemsize for a in arrays)
    return pltpu.CompilerParams(vmem_limit_bytes=grant + 2 * size)


def vmem():
    return pl.BlockSpec(memory_space=pltpu.VMEM)


def smem():
    return pl.BlockSpec(memory_space=pltpu.SMEM)


def struct(shape, dtype):
    return jax.ShapeDtypeStruct(shape, dtype)


def dims(left, right):
    return (((left,), (right,)), ((), ()))


def dot(a, b, left=1, right=0):
    return lax.dot_general(a, b, dims(left, right), preferred_element_type=f32)


def each(count, body):
    if count <= 64:
        for index in range(count):
            body(index)
    else:
        lax.fori_loop(0, count, lambda index, none: (body(index), none)[1], 0)


def start_of(index, size):
    return index * size if isinstance(index, int) else pl.multiple_of(index * size, size)


def partner(me, step, size):
    if size & (size - 1) == 0:
        return me ^ step
    return (me + step) % size


def source(me, step, size):
    if size & (size - 1) == 0:
        return me ^ step
    return (me + size - step) % size


def exchange(value, axis, step, members):
    size = lax.axis_size(axis)
    pairs = [(i, i // members * members + partner(i % members, step, members)) for i in range(size)]
    return lax.ppermute(value, axis, pairs)


def exchange_twin(value, axis, members):
    size = lax.axis_size(axis)
    return lax.ppermute(value, axis, [(i, (i + members) % size) for i in range(size)])


def band_kernel(place, limit, rows, cols, ids, values, bias, band, bias_out, sums, scaled, here, row, col, sems):
    blocks, tile, _ = sums.shape
    row_blocks = band.shape[1] // tile
    slots = rows.shape[-1]
    ids_here, values_here = here
    lanes = ids_here.shape[0] // slots
    pairs = ((ids, ids_here), (values, values_here), (rows, row), (cols, col), (bias, bias_out))
    copies = [pltpu.make_async_copy(a, b, sems.at[i]) for i, (a, b) in enumerate(pairs)]
    for copy in copies:
        copy.start()

    def clear(index):
        sums[index] = jnp.zeros((tile, tile), f32)

    each(blocks, clear)
    for copy in copies:
        copy.wait()
    line = lax.broadcasted_iota(jnp.int32, scaled.shape, 0)
    scaled[...] = jnp.where(line < limit[0, 0] * lanes, values_here[...].astype(f32), 0.0)
    which = lax.broadcasted_iota(jnp.int32, (tile, tile), 0)

    def add(slot):
        block = col[0, 0, slot] * row_blocks + row[0, 0, slot]
        dense = jnp.zeros((tile, tile), f32)
        for lane in range(lanes):
            place = pl.ds(slot * lanes + lane, 1)
            dense = jnp.where(which == ids_here[place, :], scaled[place, :], dense)
        sums[block] = sums[block] + dense

    several = next(count for count in (4, 2, 1) if slots % count == 0)

    def group(index, none):
        for other in range(several):
            add(index * several + other)
        return none

    lax.fori_loop(0, (limit[0, 0] + several - 1) // several, group, 0)

    def put(index):
        c, r = index // row_blocks, place(index % row_blocks)
        band[pl.ds(start_of(c, tile), tile), pl.ds(start_of(r, tile), tile)] = sums[index].astype(bf16)

    each(blocks, put)


def make_band(limit, rows, cols, ids, values, bias, row_blocks, col_blocks, members, twins):
    blocks_own = row_blocks // (members * twins)

    def place(block):
        owner = block // blocks_own
        return (owner % members * twins + owner // members) * blocks_own + block % blocks_own

    tile = ids.shape[-1]
    lines = ids.shape[-3] * ids.shape[-2]
    ids = ids.reshape(lines, tile)
    values = values.reshape(lines, tile)
    bias = bias.reshape(1, -1)
    out = struct((col_blocks * tile, row_blocks * tile), bf16)
    sums = struct((col_blocks * row_blocks, tile, tile), f32)
    return pl.pallas_call(
        functools.partial(band_kernel, place),
        out_shape=(out, struct(bias.shape, f32)),
        in_specs=[smem()] + [pl.BlockSpec(memory_space=pltpu.HBM)] * 5,
        out_specs=(vmem(), vmem()),
        scratch_shapes=[
            pltpu.VMEM(sums.shape, f32),
            pltpu.VMEM((lines, tile), f32),
            (pltpu.VMEM((lines, tile), jnp.int32), pltpu.VMEM((lines, tile), bf16)),
            pltpu.SMEM(rows.shape, jnp.int32),
            pltpu.SMEM(cols.shape, jnp.int32),
            pltpu.SemaphoreType.DMA((5,)),
        ],
        compiler_params=pltpu.CompilerParams(vmem_limit_bytes=grant + sums.size * 4 + out.size * 2),
        cost_estimate=pl.CostEstimate(flops=8 * sums.size * 8, bytes_accessed=8 * 2**20, transcendentals=0),
        name="band",
    )(limit, *[pltpu.with_memory_space_constraint(a, pltpu.HBM) for a in (rows, cols, ids, values, bias)])


def forward_kernel(size, *refs):
    parts, (band, kept), messages, (panel, sums) = refs[:size], refs[size : size + 2], refs[size + 2 : -2], refs[-2:]
    me = lax.axis_index("row")
    members, _, own = sums.shape
    mine = lax.rem(lax.axis_index("col"), members)
    width = parts[0].shape[0]
    for step, part in enumerate(parts):
        slot = pl.multiple_of(source(me, step, size) * width, width)
        panel[pl.ds(slot, width), :] = part[...].astype(f32)
    left = panel[...].astype(bf16)
    many = max(own, min(wide, band.shape[1]))

    def piece(index):
        got = dot(left, band[:, pl.ds(start_of(index, many), many)])
        for part in range(many // own):
            sums[index * (many // own) + part] = got[:, part * own : (part + 1) * own]

    each(band.shape[1] // many, piece)
    kept[...] = sums[mine]
    for step, message in enumerate(messages):
        message[...] = sums[partner(mine, step + 1, members)].astype(bf16)


def forward(parts, band, members):
    hidden = parts[0].shape[0] * len(parts)
    nodes, total = band.shape
    block = (hidden, total // members)
    sums = struct((members,) + block, f32)
    return pl.pallas_call(
        functools.partial(forward_kernel, len(parts)),
        out_shape=(struct(block, f32),) + (struct(block, bf16),) * (members - 1),
        in_specs=[vmem()] * (len(parts) + 1),
        out_specs=(vmem(),) * members,
        scratch_shapes=[pltpu.VMEM((hidden, nodes), f32), pltpu.VMEM(sums.shape, f32)],
        compiler_params=room(band, sums),
        name="forward",
    )(*parts, band)


def add_kernel(kept, *refs):
    parts, out = refs[:-1], refs[-1]
    total = kept[...]
    for part in parts:
        total = total + part[...].astype(f32)
    out[...] = total.astype(bf16)


def add(kept, parts):
    return pl.pallas_call(
        add_kernel,
        out_shape=struct(kept.shape, bf16),
        in_specs=[vmem()] * (len(parts) + 1),
        out_specs=vmem(),
        compiler_params=room(kept),
        name="add",
    )(kept, *parts)


def pair_rows(line):
    high = line.astype(bf16).astype(f32)
    row = lax.broadcasted_iota(jnp.int32, (tail, line.shape[1]), 0)
    return jnp.where(row == 0, high, jnp.where(row == 1, line - high, 0.0))


def apply_kernel(sums, weight, out):
    out[...] = dot(sums[...], weight[...], 0, 0)


def apply_weight(sums, weight):
    return pl.pallas_call(
        apply_kernel,
        out_shape=struct((sums.shape[1], weight.shape[1]), f32),
        in_specs=[vmem()] * 2,
        out_specs=vmem(),
        compiler_params=room(sums),
        name="apply_weight",
    )(sums, weight)


def own_kernel(members, twins, *refs):
    sums, (weight, bias, first), cotangents = refs[:twins], refs[twins : twins + 3], refs[twins + 3 : 2 * twins + 3]
    pre_out, message, wide_pre, given = refs[2 * twins + 3 :]
    mine = lax.axis_index("col") // members
    own = cotangents[0].shape[0]
    for index, part in enumerate(cotangents):
        place = mine if index == 0 else twins - 1 - mine
        given[pl.ds(pl.multiple_of(place * own, own), own), :] = part[...]
    pre = first[...]
    for part in sums[1:]:
        pre = pre + dot(part[...], weight[...], 0, 0)
    pre = pre + bias[...]
    wide_pre[...] = pre
    squashed = jax.nn.sigmoid(pre)
    grad = given[...] * squashed * (1.0 + pre * (1.0 - squashed))
    grad = grad.astype(bf16)
    rows = grad.shape[0]
    message[:rows, :] = grad
    weight_part = dot(sums[0][...], grad)
    for part in sums[1:]:
        weight_part = weight_part + dot(part[...], grad)
    message[rows:, :] = weight_part.astype(bf16)
    pre_out[...] = wide_pre[pl.ds(pl.multiple_of(mine * own, own), own), :]


def own_rows(sums, weight, bias, first, cotangents, members):
    twins = len(sums)
    hidden, rows = sums[0].shape
    own = cotangents[0].shape[0]
    return pl.pallas_call(
        functools.partial(own_kernel, members, twins),
        out_shape=(struct((own, hidden), f32), struct((rows + hidden, hidden), bf16)),
        in_specs=[vmem()] * (2 * twins + 3),
        out_specs=(vmem(),) * 2,
        scratch_shapes=[pltpu.VMEM((rows, hidden), f32), pltpu.VMEM((rows, hidden), f32)],
        compiler_params=room(*sums),
        name="own_rows",
    )(*sums, weight, bias, first, *cotangents)


def activate_kernel(pre, act):
    act[...] = pre[...] * jax.nn.sigmoid(pre[...])


def activate(pre):
    return pl.pallas_call(
        activate_kernel,
        out_shape=struct(pre.shape, f32),
        in_specs=[vmem()],
        out_specs=vmem(),
        compiler_params=room(pre),
        name="activate",
    )(pre)


def group_of(members):
    return 2 if members % 2 == 0 and members & (members - 1) == 0 else 1


def group_product(parts, first, weight, band, rows, mine, members):
    group = len(parts)
    own = rows.shape[0] // group
    base = source(mine, first, members) // group * group
    for index, part in enumerate(parts):
        spot = pl.multiple_of((source(mine, first + index, members) - base) * own, own)
        rows[pl.ds(spot, own), :] = part[:own, :]
    back = dot(weight[...], rows[...], 1, 1).astype(bf16)
    wide_own = group * own
    return dot(back, band[:, pl.ds(pl.multiple_of(base * own, wide_own), wide_own)], 1, 1)


def early_kernel(group, members, *refs):
    parts, (weight, band, out, rows) = refs[:group], refs[group:]
    mine = lax.rem(lax.axis_index("col"), members)
    out[...] = group_product(parts, 0, weight, band, rows, mine, members)


def backward_kernel(size, group, members, *refs):
    got, (weight, band, early), messages = refs[:members], refs[members : members + 3], refs[members + 3 :][:size]
    kept, rows, slots, lines, grads, packed = refs[members + 3 + size :]
    hidden = weight.shape[0]
    own = got[0].shape[0] - hidden
    width, nodes = kept.shape
    me = lax.axis_index("row")
    mine = lax.rem(lax.axis_index("col"), members)
    for step, part in enumerate(got):
        place = source(mine, step, members)
        slots[place] = part[own:, :].astype(f32)
        lines[place] = jnp.sum(part[:own, :].astype(f32), axis=0, keepdims=True)
    weight_part, bias_part = slots[0], lines[0]
    for index in range(1, members):
        weight_part = weight_part + slots[index]
        bias_part = bias_part + lines[index]
    total = early[...]
    for first in range(group, members, group):
        total = total + group_product(got[first : first + group], first, weight, band, rows, mine, members)
    grads[...] = total
    split = nodes // hidden
    packed[split * width : split * width + hidden, :] = weight_part
    packed[split * width + hidden :, :] = pair_rows(bias_part)
    for step in range(size):
        slot = pl.multiple_of(partner(me, step, size) * width, width)
        block = grads[pl.ds(slot, width), :]
        if step == 0:
            kept[...] = block
        for index in range(split):
            packed[index * width : (index + 1) * width, :] = block[:, index * hidden : (index + 1) * hidden]
        messages[step][...] = packed[...].astype(bf16)


def backward(got, weight, band, size):
    members = len(got)
    group = group_of(members)
    hidden = weight.shape[0]
    nodes, total = band.shape
    width = hidden // size
    rows = pltpu.VMEM((total // members * group, hidden), bf16)
    early = pl.pallas_call(
        functools.partial(early_kernel, group, members),
        out_shape=struct((hidden, nodes), f32),
        in_specs=[vmem()] * (group + 2),
        out_specs=vmem(),
        scratch_shapes=[rows],
        compiler_params=room(band, *got),
        name="early",
    )(*got[:group], weight, band)
    message = struct((width * (nodes // hidden) + hidden + tail, hidden), bf16)
    return pl.pallas_call(
        functools.partial(backward_kernel, size, group, members),
        out_shape=(message,) * size + (struct((width, nodes), f32),),
        in_specs=[vmem()] * (members + 3),
        out_specs=(vmem(),) * (size + 1),
        scratch_shapes=[
            rows,
            pltpu.VMEM((members, hidden, hidden), f32),
            pltpu.VMEM((members, 1, hidden), f32),
            pltpu.VMEM((hidden, nodes), f32),
            pltpu.VMEM(message.shape, f32),
        ],
        compiler_params=room(band, *got),
        name="backward",
    )(*got, weight, band, early)


def final_kernel(size, shrink, *refs):
    messages, (kept, features, weight, bias, slots) = refs[:size], refs[size:]
    width, nodes = kept.shape
    hidden = weight.shape[0]
    split = nodes // hidden
    me = lax.axis_index("row")
    for step, message in enumerate(messages):
        slots[source(me, step, size)] = message[split * width :, :].astype(f32)
    for index in range(split):
        place = slice(index * hidden, (index + 1) * hidden)
        total = kept[:, place]
        for message in messages[1:]:
            total = total + message[index * width : (index + 1) * width, :].astype(f32)
        features[:, place] = total.astype(bf16)
    total = slots[0]
    for index in range(1, size):
        total = total + slots[index]
    weight[...] = total[:hidden] * shrink
    bias[...] = jnp.sum(total[hidden:], axis=0, keepdims=True) * shrink


def final(messages, kept, hidden, shrink):
    width, nodes = kept.shape
    size = len(messages)
    return pl.pallas_call(
        functools.partial(final_kernel, size, shrink),
        out_shape=(struct((width, nodes), bf16), struct((hidden, hidden), f32), struct((1, hidden), f32)),
        in_specs=[vmem()] * (size + 1),
        out_specs=(vmem(),) * 3,
        scratch_shapes=[pltpu.VMEM((size, hidden + tail, hidden), f32)],
        compiler_params=room(*messages),
        name="final",
    )(*messages, kept)


def shards(
    features,
    weight,
    bias_vector,
    tile_rows,
    tile_cols,
    neighbours,
    edge_weights,
    tile_count,
    cotangent,
):
    tile_size = neighbours.shape[-1]
    hidden = weight.shape[1]
    size, owners = lax.axis_size("row"), lax.axis_size("col")
    twins = 2 if owners % 2 == 0 else 1
    members = owners // twins
    blocks_own = cotangent.shape[0] // tile_size
    row_blocks = blocks_own * owners
    col_blocks = blocks_own * size
    turned = features.T
    parts = [turned] + [exchange(turned, "row", step, size) for step in range(1, size)]
    band, bias = make_band(
        tile_count, tile_rows, tile_cols, neighbours, edge_weights, bias_vector, row_blocks, col_blocks, members, twins
    )
    kept, *messages = forward(parts, band, members)
    got = [exchange(message, "col", step + 1, members) for step, message in enumerate(messages)]
    cotangents = [cotangent]
    if twins > 1:
        other, messages[0] = lax.optimization_barrier((cotangent, messages[0]))
        cotangents.append(exchange_twin(other, "col", members))
    sums = [add(kept, got)]
    if twins > 1:
        sums.append(exchange_twin(sums[0], "col", members))
    first = apply_weight(sums[0], weight)
    pre, message = own_rows(sums, weight, bias, first, cotangents, members)
    activations = activate(pre)
    got = [message] + [exchange(message, "col", step, members) for step in range(1, members)]
    *messages, kept = backward(got, weight, band, size)
    messages = [messages[0]] + [exchange(messages[step], "row", step, size) for step in range(1, size)]
    node_count = cotangent.shape[0] * size * owners
    grad_features, grad_weight, grad_bias = final(messages, kept, hidden, float(node_count) ** (-0.5))
    return (activations, grad_features.T, grad_weight, grad_bias.reshape(hidden))


def solution(mesh):
    in_specs = (
        P("col", "row"),
        P(),
        P(),
        P("row", "col", None),
        P("row", "col", None),
        P("row", "col", None, None, None),
        P("row", "col", None, None, None),
        P("row", "col"),
        P(("row", "col"), None),
    )
    out_specs = (P(("row", "col"), None), P("col", "row"), P(), P())
    return jax.shard_map(shards, mesh=mesh, in_specs=in_specs, out_specs=out_specs, check_vma=False)
```

```python
import functools

import jax
import jax.numpy as jnp
from jax import lax
from jax.experimental import pallas as pl
from jax.experimental.pallas import tpu as pltpu
from jax.sharding import PartitionSpec as P

f32 = jnp.float32
bf16 = jnp.bfloat16
tail = 16
wide = 1024
grant = 8 * 2**20


def room(*arrays):
    size = sum(a.size * a.dtype.itemsize for a in arrays)
    return pltpu.CompilerParams(vmem_limit_bytes=grant + 2 * size)


def vmem():
    return pl.BlockSpec(memory_space=pltpu.VMEM)


def smem():
    return pl.BlockSpec(memory_space=pltpu.SMEM)


def struct(shape, dtype):
    return jax.ShapeDtypeStruct(shape, dtype)


def dims(left, right):
    return (((left,), (right,)), ((), ()))


def dot(a, b, left=1, right=0):
    return lax.dot_general(a, b, dims(left, right), preferred_element_type=f32)


def each(count, body):
    if count <= 64:
        for index in range(count):
            body(index)
    else:
        lax.fori_loop(0, count, lambda index, none: (body(index), none)[1], 0)


def start_of(index, size):
    return index * size if isinstance(index, int) else pl.multiple_of(index * size, size)


def partner(me, step, size):
    if size & (size - 1) == 0:
        return me ^ step
    return (me + step) % size


def source(me, step, size):
    if size & (size - 1) == 0:
        return me ^ step
    return (me + size - step) % size


def exchange(value, axis, step, members):
    size = lax.axis_size(axis)
    pairs = [(i, i // members * members + partner(i % members, step, members)) for i in range(size)]
    return lax.ppermute(value, axis, pairs)


def exchange_twin(value, axis, members):
    size = lax.axis_size(axis)
    return lax.ppermute(value, axis, [(i, (i + members) % size) for i in range(size)])


def band_kernel(place, limit, rows, cols, ids, values, bias, band, bias_out, sums, scaled, here, row, col, sems):
    blocks, tile, _ = sums.shape
    row_blocks = band.shape[1] // tile
    slots = rows.shape[-1]
    ids_here, values_here = here
    lanes = ids_here.shape[0] // slots
    pairs = ((ids, ids_here), (values, values_here), (rows, row), (cols, col), (bias, bias_out))
    copies = [pltpu.make_async_copy(a, b, sems.at[i]) for i, (a, b) in enumerate(pairs)]
    for copy in copies:
        copy.start()

    def clear(index):
        sums[index] = jnp.zeros((tile, tile), f32)

    each(blocks, clear)
    for copy in copies:
        copy.wait()
    line = lax.broadcasted_iota(jnp.int32, scaled.shape, 0)
    scaled[...] = jnp.where(line < limit[0, 0] * lanes, values_here[...].astype(f32), 0.0)
    which = lax.broadcasted_iota(jnp.int32, (tile, tile), 0)

    def add(slot):
        block = col[0, 0, slot] * row_blocks + row[0, 0, slot]
        dense = jnp.zeros((tile, tile), f32)
        for lane in range(lanes):
            place = pl.ds(slot * lanes + lane, 1)
            dense = jnp.where(which == ids_here[place, :], scaled[place, :], dense)
        sums[block] = sums[block] + dense

    several = next(count for count in (4, 2, 1) if slots % count == 0)

    def group(index, none):
        for other in range(several):
            add(index * several + other)
        return none

    lax.fori_loop(0, (limit[0, 0] + several - 1) // several, group, 0)

    def put(index):
        c, r = index // row_blocks, place(index % row_blocks)
        band[pl.ds(start_of(c, tile), tile), pl.ds(start_of(r, tile), tile)] = sums[index].astype(bf16)

    each(blocks, put)


def make_band(limit, rows, cols, ids, values, bias, row_blocks, col_blocks, members, twins):
    blocks_own = row_blocks // (members * twins)

    def place(block):
        owner = block // blocks_own
        return (owner % members * twins + owner // members) * blocks_own + block % blocks_own

    tile = ids.shape[-1]
    lines = ids.shape[-3] * ids.shape[-2]
    ids = ids.reshape(lines, tile)
    values = values.reshape(lines, tile)
    bias = bias.reshape(1, -1)
    out = struct((col_blocks * tile, row_blocks * tile), bf16)
    sums = struct((col_blocks * row_blocks, tile, tile), f32)
    return pl.pallas_call(
        functools.partial(band_kernel, place),
        out_shape=(out, struct(bias.shape, f32)),
        in_specs=[smem()] + [pl.BlockSpec(memory_space=pltpu.HBM)] * 5,
        out_specs=(vmem(), vmem()),
        scratch_shapes=[
            pltpu.VMEM(sums.shape, f32),
            pltpu.VMEM((lines, tile), f32),
            (pltpu.VMEM((lines, tile), jnp.int32), pltpu.VMEM((lines, tile), bf16)),
            pltpu.SMEM(rows.shape, jnp.int32),
            pltpu.SMEM(cols.shape, jnp.int32),
            pltpu.SemaphoreType.DMA((5,)),
        ],
        compiler_params=pltpu.CompilerParams(vmem_limit_bytes=grant + sums.size * 4 + out.size * 2),
        cost_estimate=pl.CostEstimate(flops=8 * sums.size * 8, bytes_accessed=8 * 2**20, transcendentals=0),
        name="band",
    )(limit, *[pltpu.with_memory_space_constraint(a, pltpu.HBM) for a in (rows, cols, ids, values, bias)])


def forward_kernel(size, members, *refs):
    parts, (band, kept), messages, panel = refs[:size], refs[size : size + 2], refs[size + 2 : -1], refs[-1]
    me = lax.axis_index("row")
    mine = lax.rem(lax.axis_index("col"), members)
    width = parts[0].shape[0]
    own = kept.shape[1]
    for step, part in enumerate(parts):
        slot = pl.multiple_of(source(me, step, size) * width, width)
        panel[pl.ds(slot, width), :] = part[...].astype(panel.dtype)
    left = panel[...].astype(bf16)
    for step, message in enumerate((kept,) + messages):
        columns = pl.ds(pl.multiple_of(partner(mine, step, members) * own, own), own)
        message[...] = dot(left, band[:, columns]).astype(message.dtype)


def forward(parts, band, members):
    width = parts[0].shape[0]
    hidden = width * len(parts)
    nodes, total = band.shape
    block = (hidden, total // members)
    panel = pltpu.VMEM((hidden, nodes), bf16 if width % 16 == 0 else f32)
    return pl.pallas_call(
        functools.partial(forward_kernel, len(parts), members),
        out_shape=(struct(block, f32),) + (struct(block, bf16),) * (members - 1),
        in_specs=[vmem()] * (len(parts) + 1),
        out_specs=(vmem(),) * members,
        scratch_shapes=[panel],
        compiler_params=room(band),
        name="forward",
    )(*parts, band)


def add_kernel(kept, *refs):
    parts, out = refs[:-1], refs[-1]
    total = kept[...]
    for part in parts:
        total = total + part[...].astype(f32)
    out[...] = total.astype(bf16)


def add(kept, parts):
    return pl.pallas_call(
        add_kernel,
        out_shape=struct(kept.shape, bf16),
        in_specs=[vmem()] * (len(parts) + 1),
        out_specs=vmem(),
        compiler_params=room(kept),
        name="add",
    )(kept, *parts)


def pair_rows(line):
    high = line.astype(bf16).astype(f32)
    row = lax.broadcasted_iota(jnp.int32, (tail, line.shape[1]), 0)
    return jnp.where(row == 0, high, jnp.where(row == 1, line - high, 0.0))


def apply_kernel(sums, weight, out):
    out[...] = dot(sums[...], weight[...], 0, 0)


def apply_weight(sums, weight):
    return pl.pallas_call(
        apply_kernel,
        out_shape=struct((sums.shape[1], weight.shape[1]), f32),
        in_specs=[vmem()] * 2,
        out_specs=vmem(),
        compiler_params=room(sums),
        name="apply_weight",
    )(sums, weight)


def own_kernel(members, twins, *refs):
    sums, (weight, bias, first), cotangents = refs[:twins], refs[twins : twins + 3], refs[twins + 3 : 2 * twins + 3]
    pre_out, message, wide_pre, given = refs[2 * twins + 3 :]
    mine = lax.axis_index("col") // members
    own = cotangents[0].shape[0]
    for index, part in enumerate(cotangents):
        place = mine if index == 0 else twins - 1 - mine
        given[pl.ds(pl.multiple_of(place * own, own), own), :] = part[...]
    pre = first[...]
    for part in sums[1:]:
        pre = pre + dot(part[...], weight[...], 0, 0)
    pre = pre + bias[...]
    wide_pre[...] = pre
    squashed = jax.nn.sigmoid(pre)
    grad = given[...] * squashed * (1.0 + pre * (1.0 - squashed))
    grad = grad.astype(bf16)
    rows = grad.shape[0]
    message[:rows, :] = grad
    weight_part = dot(sums[0][...], grad)
    for part in sums[1:]:
        weight_part = weight_part + dot(part[...], grad)
    message[rows:, :] = weight_part.astype(bf16)
    pre_out[...] = wide_pre[pl.ds(pl.multiple_of(mine * own, own), own), :]


def own_rows(sums, weight, bias, first, cotangents, members):
    twins = len(sums)
    hidden, rows = sums[0].shape
    own = cotangents[0].shape[0]
    return pl.pallas_call(
        functools.partial(own_kernel, members, twins),
        out_shape=(struct((own, hidden), f32), struct((rows + hidden, hidden), bf16)),
        in_specs=[vmem()] * (2 * twins + 3),
        out_specs=(vmem(),) * 2,
        scratch_shapes=[pltpu.VMEM((rows, hidden), f32), pltpu.VMEM((rows, hidden), f32)],
        compiler_params=room(*sums),
        name="own_rows",
    )(*sums, weight, bias, first, *cotangents)


def activate_kernel(pre, act):
    act[...] = pre[...] * jax.nn.sigmoid(pre[...])


def activate(pre):
    return pl.pallas_call(
        activate_kernel,
        out_shape=struct(pre.shape, f32),
        in_specs=[vmem()],
        out_specs=vmem(),
        compiler_params=room(pre),
        name="activate",
    )(pre)


def group_of(members):
    return 2 if members % 2 == 0 and members & (members - 1) == 0 else 1


def group_product(parts, first, weight, band, rows, mine, members):
    group = len(parts)
    own = rows.shape[0] // group
    base = source(mine, first, members) // group * group
    for index, part in enumerate(parts):
        spot = pl.multiple_of((source(mine, first + index, members) - base) * own, own)
        rows[pl.ds(spot, own), :] = part[:own, :]
    back = dot(weight[...], rows[...], 1, 1).astype(bf16)
    wide_own = group * own
    return dot(back, band[:, pl.ds(pl.multiple_of(base * own, wide_own), wide_own)], 1, 1)


def early_kernel(group, members, *refs):
    parts, (weight, band, out, rows) = refs[:group], refs[group:]
    mine = lax.rem(lax.axis_index("col"), members)
    out[...] = group_product(parts, 0, weight, band, rows, mine, members)


def backward_kernel(order, size, group, members, *refs):
    given, (weight, band, early), messages = refs[:members], refs[members : members + 3], refs[members + 3 :][:size]
    kept, rows, slots, lines, grads, packed = refs[members + 3 + size :]
    got = [given[order.index(step)] for step in range(members)]
    hidden = weight.shape[0]
    own = got[0].shape[0] - hidden
    width, nodes = kept.shape
    me = lax.axis_index("row")
    mine = lax.rem(lax.axis_index("col"), members)
    for step, part in enumerate(got):
        place = source(mine, step, members)
        slots[place] = part[own:, :].astype(f32)
        lines[place] = jnp.sum(part[:own, :].astype(f32), axis=0, keepdims=True)
    weight_part, bias_part = slots[0], lines[0]
    for index in range(1, members):
        weight_part = weight_part + slots[index]
        bias_part = bias_part + lines[index]
    total = early[...]
    for first in range(group, members, group):
        total = total + group_product(got[first : first + group], first, weight, band, rows, mine, members)
    grads[...] = total
    split = nodes // hidden
    packed[split * width : split * width + hidden, :] = weight_part
    packed[split * width + hidden :, :] = pair_rows(bias_part)
    for step in range(size):
        slot = pl.multiple_of(partner(me, step, size) * width, width)
        block = grads[pl.ds(slot, width), :]
        if step == 0:
            kept[...] = block
        for index in range(split):
            packed[index * width : (index + 1) * width, :] = block[:, index * hidden : (index + 1) * hidden]
        messages[step][...] = packed[...].astype(bf16)


def backward(got, weight, band, size):
    members = len(got)
    group = group_of(members)
    order = [0, *range(2, members), 1][:members]
    hidden = weight.shape[0]
    nodes, total = band.shape
    width = hidden // size
    rows = pltpu.VMEM((total // members * group, hidden), bf16)
    early = pl.pallas_call(
        functools.partial(early_kernel, group, members),
        out_shape=struct((hidden, nodes), f32),
        in_specs=[vmem()] * (group + 2),
        out_specs=vmem(),
        scratch_shapes=[rows],
        compiler_params=room(band, *got),
        name="early",
    )(*got[:group], weight, band)
    message = struct((width * (nodes // hidden) + hidden + tail, hidden), bf16)
    return pl.pallas_call(
        functools.partial(backward_kernel, order, size, group, members),
        out_shape=(message,) * size + (struct((width, nodes), f32),),
        in_specs=[vmem()] * (members + 3),
        out_specs=(vmem(),) * (size + 1),
        scratch_shapes=[
            rows,
            pltpu.VMEM((members, hidden, hidden), f32),
            pltpu.VMEM((members, 1, hidden), f32),
            pltpu.VMEM((hidden, nodes), f32),
            pltpu.VMEM(message.shape, f32),
        ],
        compiler_params=room(band, *got),
        name="backward",
    )(*[got[step] for step in order], weight, band, early)


def final_kernel(order, size, shrink, *refs):
    given, (kept, features_out, weight_out, bias_out, slots, features, weight, bias, sems) = refs[:size], refs[size:]
    width, nodes = kept.shape
    hidden = weight.shape[0]
    split = nodes // hidden
    me = lax.axis_index("row")
    messages = [given[order.index(step)] for step in range(size)]
    pairs = ((weight, weight_out), (bias, bias_out), (features, features_out))
    copies = [pltpu.make_async_copy(a, b, sems.at[i]) for i, (a, b) in enumerate(pairs)]
    for step, message in enumerate(messages):
        slots[source(me, step, size)] = message[split * width :, :].astype(f32)
    total = slots[0]
    for index in range(1, size):
        total = total + slots[index]
    weight[...] = total[:hidden] * shrink
    copies[0].start()
    bias[...] = jnp.sum(total[hidden:], axis=0, keepdims=True) * shrink
    copies[1].start()
    for index in range(split):
        place = slice(index * hidden, (index + 1) * hidden)
        total = kept[:, place]
        for message in messages[1:]:
            total = total + message[index * width : (index + 1) * width, :].astype(f32)
        features[:, place] = total.astype(bf16)
    copies[2].start()
    for copy in copies:
        copy.wait()


def final(messages, kept, hidden, shrink):
    width, nodes = kept.shape
    size = len(messages)
    order = [0, *range(size - 1, 0, -1)]
    outs = (struct((width, nodes), bf16), struct((hidden, hidden), f32), struct((1, hidden), f32))
    return pl.pallas_call(
        functools.partial(final_kernel, order, size, shrink),
        out_shape=outs,
        in_specs=[vmem()] * (size + 1),
        out_specs=(pl.BlockSpec(memory_space=pltpu.HBM),) * 3,
        scratch_shapes=[pltpu.VMEM((size, hidden + tail, hidden), f32)]
        + [pltpu.VMEM(out.shape, out.dtype) for out in outs]
        + [pltpu.SemaphoreType.DMA((3,))],
        compiler_params=room(*messages),
        name="final",
    )(*[messages[step] for step in order], kept)


def shards(
    features,
    weight,
    bias_vector,
    tile_rows,
    tile_cols,
    neighbours,
    edge_weights,
    tile_count,
    cotangent,
):
    tile_size = neighbours.shape[-1]
    hidden = weight.shape[1]
    size, owners = lax.axis_size("row"), lax.axis_size("col")
    twins = 2 if owners % 2 == 0 else 1
    members = owners // twins
    blocks_own = cotangent.shape[0] // tile_size
    row_blocks = blocks_own * owners
    col_blocks = blocks_own * size
    turned = features.T
    parts = [turned] + [exchange(turned, "row", step, size) for step in range(1, size)]
    band, bias = make_band(
        tile_count, tile_rows, tile_cols, neighbours, edge_weights, bias_vector, row_blocks, col_blocks, members, twins
    )
    kept, *messages = forward(parts, band, members)
    got = [exchange(message, "col", step + 1, members) for step, message in enumerate(messages)]
    cotangents = [cotangent]
    if twins > 1:
        other, messages[0] = lax.optimization_barrier((cotangent, messages[0]))
        cotangents.append(exchange_twin(other, "col", members))
    sums = [add(kept, got[::-1])]
    if twins > 1:
        sums.append(exchange_twin(sums[0], "col", members))
    first = apply_weight(sums[0], weight)
    pre, message = own_rows(sums, weight, bias, first, cotangents, members)
    activations = activate(pre)
    got = [message] + [exchange(message, "col", step, members) for step in range(1, members)]
    *messages, kept = backward(got, weight, band, size)
    messages = [messages[0]] + [exchange(messages[step], "row", step, size) for step in range(1, size)]
    node_count = cotangent.shape[0] * size * owners
    grad_features, grad_weight, grad_bias = final(messages, kept, hidden, float(node_count) ** (-0.5))
    return (activations, grad_features.T, grad_weight, grad_bias.reshape(hidden))


def solution(mesh):
    in_specs = (
        P("col", "row"),
        P(),
        P(),
        P("row", "col", None),
        P("row", "col", None),
        P("row", "col", None, None, None),
        P("row", "col", None, None, None),
        P("row", "col"),
        P(("row", "col"), None),
    )
    out_specs = (P(("row", "col"), None), P("col", "row"), P(), P())
    return jax.shard_map(shards, mesh=mesh, in_specs=in_specs, out_specs=out_specs, check_vma=False)
```

```python
import functools

import jax
import jax.numpy as jnp
from jax import lax
from jax.experimental import pallas as pl
from jax.experimental.pallas import tpu as pltpu
from jax.sharding import PartitionSpec as P

f32 = jnp.float32
bf16 = jnp.bfloat16
i16 = jnp.int16
levels = 32736.0
tail = 16
wide = 1024
grant = 8 * 2**20


def room(*arrays):
    size = sum(a.size * a.dtype.itemsize for a in arrays)
    return pltpu.CompilerParams(vmem_limit_bytes=grant + 2 * size)


def vmem():
    return pl.BlockSpec(memory_space=pltpu.VMEM)


def smem():
    return pl.BlockSpec(memory_space=pltpu.SMEM)


def struct(shape, dtype):
    return jax.ShapeDtypeStruct(shape, dtype)


def dims(left, right):
    return (((left,), (right,)), ((), ()))


def dot(a, b, left=1, right=0):
    return lax.dot_general(a, b, dims(left, right), preferred_element_type=f32)


def each(count, body):
    if count <= 64:
        for index in range(count):
            body(index)
    else:
        lax.fori_loop(0, count, lambda index, none: (body(index), none)[1], 0)


def start_of(index, size):
    return index * size if isinstance(index, int) else pl.multiple_of(index * size, size)


def code(value, out):
    rows = value.shape[0]
    top = jnp.max(jnp.max(jnp.abs(value), axis=0, keepdims=True), axis=1, keepdims=True)
    power = jnp.ceil(jnp.log2(jnp.maximum(top, 1e-20)))
    power = jnp.broadcast_to(power, (1, value.shape[1]))
    out[:rows, :] = jnp.round(value * (jnp.exp2(-power) * levels)).astype(jnp.int32).astype(i16)
    out[rows:, :] = jnp.broadcast_to(power, (tail, value.shape[1])).astype(jnp.int32).astype(i16)


def decode(part):
    whole = part[...].astype(jnp.int32).astype(f32)
    rows = whole.shape[0] - tail
    return whole[:rows] * (jnp.exp2(whole[rows : rows + 1]) * (1.0 / levels))


def partner(me, step, size):
    if size & (size - 1) == 0:
        return me ^ step
    return (me + step) % size


def source(me, step, size):
    if size & (size - 1) == 0:
        return me ^ step
    return (me + size - step) % size


def exchange(value, axis, step, members):
    size = lax.axis_size(axis)
    pairs = [(i, i // members * members + partner(i % members, step, members)) for i in range(size)]
    return lax.ppermute(value, axis, pairs)


def exchange_twin(value, axis, members):
    size = lax.axis_size(axis)
    return lax.ppermute(value, axis, [(i, (i + members) % size) for i in range(size)])


def band_kernel(
    place, limit, rows, cols, ids, values, bias, cotangent, band, bias_out, longer, sums, scaled, here, row, col, sems
):
    blocks, tile, _ = sums.shape
    row_blocks = band.shape[1] // tile
    slots = rows.shape[-1]
    ids_here, values_here = here
    lanes = ids_here.shape[0] // slots
    pairs = ((ids, ids_here), (values, values_here), (rows, row), (cols, col), (bias, bias_out))
    pairs = pairs + ((cotangent, longer.at[pl.ds(0, cotangent.shape[0]), :]),)
    copies = [pltpu.make_async_copy(a, b, sems.at[i]) for i, (a, b) in enumerate(pairs)]
    for copy in copies:
        copy.start()
    longer[cotangent.shape[0] :, :] = jnp.zeros((tail, cotangent.shape[1]), f32)

    def clear(index):
        sums[index] = jnp.zeros((tile, tile), f32)

    each(blocks, clear)
    for copy in copies:
        copy.wait()
    line = lax.broadcasted_iota(jnp.int32, scaled.shape, 0)
    scaled[...] = jnp.where(line < limit[0, 0] * lanes, values_here[...].astype(f32), 0.0)
    which = lax.broadcasted_iota(jnp.int32, (tile, tile), 0)

    def add(slot):
        block = col[0, 0, slot] * row_blocks + row[0, 0, slot]
        dense = jnp.zeros((tile, tile), f32)
        for lane in range(lanes):
            place = pl.ds(slot * lanes + lane, 1)
            dense = jnp.where(which == ids_here[place, :], scaled[place, :], dense)
        sums[block] = sums[block] + dense

    several = next(count for count in (4, 2, 1) if slots % count == 0)

    def group(index, none):
        for other in range(several):
            add(index * several + other)
        return none

    lax.fori_loop(0, (limit[0, 0] + several - 1) // several, group, 0)

    def put(index):
        c, r = index // row_blocks, place(index % row_blocks)
        band[pl.ds(start_of(c, tile), tile), pl.ds(start_of(r, tile), tile)] = sums[index].astype(bf16)

    each(blocks, put)


def make_band(limit, rows, cols, ids, values, bias, cotangent, row_blocks, col_blocks, members, twins):
    blocks_own = row_blocks // (members * twins)

    def place(block):
        owner = block // blocks_own
        return (owner % members * twins + owner // members) * blocks_own + block % blocks_own

    tile = ids.shape[-1]
    lines = ids.shape[-3] * ids.shape[-2]
    ids = ids.reshape(lines, tile)
    values = values.reshape(lines, tile)
    bias = bias.reshape(1, -1)
    out = struct((col_blocks * tile, row_blocks * tile), bf16)
    sums = struct((col_blocks * row_blocks, tile, tile), f32)
    return pl.pallas_call(
        functools.partial(band_kernel, place),
        out_shape=(out, struct(bias.shape, f32), struct((cotangent.shape[0] + tail, cotangent.shape[1]), f32)),
        in_specs=[smem()] + [pl.BlockSpec(memory_space=pltpu.HBM)] * 6,
        out_specs=(vmem(),) * 3,
        scratch_shapes=[
            pltpu.VMEM(sums.shape, f32),
            pltpu.VMEM((lines, tile), f32),
            (pltpu.VMEM((lines, tile), jnp.int32), pltpu.VMEM((lines, tile), bf16)),
            pltpu.SMEM(rows.shape, jnp.int32),
            pltpu.SMEM(cols.shape, jnp.int32),
            pltpu.SemaphoreType.DMA((6,)),
        ],
        compiler_params=pltpu.CompilerParams(vmem_limit_bytes=grant + sums.size * 4 + out.size * 2),
        cost_estimate=pl.CostEstimate(flops=8 * sums.size * 8, bytes_accessed=8 * 2**20, transcendentals=0),
        name="band",
    )(limit, *[pltpu.with_memory_space_constraint(a, pltpu.HBM) for a in (rows, cols, ids, values, bias, cotangent)])


def forward_kernel(size, members, *refs):
    parts, (band, kept), messages, panel = refs[:size], refs[size : size + 2], refs[size + 2 : -1], refs[-1]
    me = lax.axis_index("row")
    mine = lax.rem(lax.axis_index("col"), members)
    width = parts[0].shape[0]
    own = kept.shape[1]
    for step, part in enumerate(parts):
        slot = pl.multiple_of(source(me, step, size) * width, width)
        panel[pl.ds(slot, width), :] = part[...].astype(panel.dtype)
    left = panel[...].astype(bf16)
    for step, message in enumerate((kept,) + messages):
        columns = pl.ds(pl.multiple_of(partner(mine, step, members) * own, own), own)
        got = dot(left, band[:, columns])
        if step == 0:
            kept[...] = got
        else:
            code(got, message)


def forward(parts, band, members):
    width = parts[0].shape[0]
    hidden = width * len(parts)
    nodes, total = band.shape
    block = (hidden, total // members)
    panel = pltpu.VMEM((hidden, nodes), bf16 if width % 16 == 0 else f32)
    return pl.pallas_call(
        functools.partial(forward_kernel, len(parts), members),
        out_shape=(struct(block, f32),) + (struct((hidden + tail, block[1]), i16),) * (members - 1),
        in_specs=[vmem()] * (len(parts) + 1),
        out_specs=(vmem(),) * members,
        scratch_shapes=[panel],
        compiler_params=room(band),
        name="forward",
    )(*parts, band)


def add_kernel(kept, *refs):
    parts, out = refs[:-1], refs[-1]
    total = kept[...]
    for part in parts:
        total = total + decode(part)
    code(total, out)


def add(kept, parts):
    return pl.pallas_call(
        add_kernel,
        out_shape=struct((kept.shape[0] + tail, kept.shape[1]), i16),
        in_specs=[vmem()] * (len(parts) + 1),
        out_specs=vmem(),
        compiler_params=room(kept),
        name="add",
    )(kept, *parts)


def pair_rows(line):
    high = line.astype(bf16).astype(f32)
    row = lax.broadcasted_iota(jnp.int32, (tail, line.shape[1]), 0)
    return jnp.where(row == 0, high, jnp.where(row == 1, line - high, 0.0))


def parts_of(value):
    high = value.astype(bf16)
    return high, (value - high.astype(f32)).astype(bf16)


def apply(value, weight):
    high, low = parts_of(value)
    return dot(high, weight[...], 0, 0) + dot(low, weight[...], 0, 0)


def before_kernel(members, twins, *refs):
    cotangents, (sums, weight, whole, first, given) = refs[:twins], refs[twins:]
    mine = lax.axis_index("col") // members
    own = cotangents[0].shape[0]
    for index, part in enumerate(cotangents):
        place = mine if index == 0 else twins - 1 - mine
        given[pl.ds(pl.multiple_of(place * own, own), own), :] = part[:own, :]
    value = decode(sums)
    whole[...] = value
    first[...] = apply(value, weight)


def before(cotangents, sums, weight, members):
    hidden, rows = sums.shape[0] - tail, sums.shape[1]
    product = struct((rows, weight.shape[1]), f32)
    return pl.pallas_call(
        functools.partial(before_kernel, members, len(cotangents)),
        out_shape=(struct((hidden, rows), f32), product, product),
        in_specs=[vmem()] * (len(cotangents) + 2),
        out_specs=(vmem(),) * 3,
        compiler_params=room(sums),
        name="before",
    )(*cotangents, sums, weight)


def own_kernel(weight, bias, whole, first, given, *refs):
    others, (pre_out, message) = refs[:-2], refs[-2:]
    total, pre = whole[...], first[...]
    for part in others:
        value = decode(part)
        total = total + value
        pre = pre + apply(value, weight)
    pre = pre + bias[...]
    pre_out[...] = pre
    squashed = jax.nn.sigmoid(pre)
    grad = given[...] * squashed * (1.0 + pre * (1.0 - squashed))
    grad = grad.astype(bf16)
    rows = grad.shape[0]
    message[:rows, :] = grad
    high, low = parts_of(total)
    message[rows:, :] = (dot(high, grad) + dot(low, grad)).astype(bf16)


def own_rows(whole, first, given, weight, bias, others):
    hidden, rows = whole.shape
    return pl.pallas_call(
        own_kernel,
        out_shape=(struct((rows, hidden), f32), struct((rows + hidden, hidden), bf16)),
        in_specs=[vmem()] * (5 + len(others)),
        out_specs=(vmem(),) * 2,
        compiler_params=room(whole),
        name="own_rows",
    )(weight, bias, whole, first, given, *others)


def activate_kernel(members, pre, act):
    own = act.shape[0]
    mine = lax.axis_index("col") // members
    kept = pre[pl.ds(pl.multiple_of(mine * own, own), own), :]
    act[...] = kept * jax.nn.sigmoid(kept)


def activate(pre, own, members):
    return pl.pallas_call(
        functools.partial(activate_kernel, members),
        out_shape=struct((own, pre.shape[1]), f32),
        in_specs=[vmem()],
        out_specs=vmem(),
        compiler_params=room(pre),
        name="activate",
    )(pre)


def group_of(members):
    return 2 if members % 2 == 0 and members & (members - 1) == 0 else 1


def group_product(parts, first, weight, band, rows, mine, members):
    group = len(parts)
    own = rows.shape[0] // group
    base = source(mine, first, members) // group * group
    for index, part in enumerate(parts):
        spot = pl.multiple_of((source(mine, first + index, members) - base) * own, own)
        rows[pl.ds(spot, own), :] = part[:own, :]
    back = dot(weight[...], rows[...], 1, 1).astype(bf16)
    wide_own = group * own
    return dot(back, band[:, pl.ds(pl.multiple_of(base * own, wide_own), wide_own)], 1, 1)


def early_kernel(group, members, *refs):
    parts, (weight, band, out, rows) = refs[:group], refs[group:]
    mine = lax.rem(lax.axis_index("col"), members)
    out[...] = group_product(parts, 0, weight, band, rows, mine, members)


def backward_kernel(order, size, group, members, *refs):
    given, (weight, band, early), messages = refs[:members], refs[members : members + 3], refs[members + 3 :][:size]
    kept, rows, slots, lines, grads, packed = refs[members + 3 + size :]
    got = [given[order.index(step)] for step in range(members)]
    hidden = weight.shape[0]
    own = got[0].shape[0] - hidden
    width, nodes = kept.shape
    me = lax.axis_index("row")
    mine = lax.rem(lax.axis_index("col"), members)
    for step, part in enumerate(got):
        place = source(mine, step, members)
        slots[place] = part[own:, :].astype(f32)
        lines[place] = jnp.sum(part[:own, :].astype(f32), axis=0, keepdims=True)
    weight_part, bias_part = slots[0], lines[0]
    for index in range(1, members):
        weight_part = weight_part + slots[index]
        bias_part = bias_part + lines[index]
    total = early[...]
    for first in range(group, members, group):
        total = total + group_product(got[first : first + group], first, weight, band, rows, mine, members)
    grads[...] = total
    split = nodes // hidden
    packed[split * width : split * width + hidden, :] = weight_part
    packed[split * width + hidden :, :] = pair_rows(bias_part)
    for step in range(size):
        slot = pl.multiple_of(partner(me, step, size) * width, width)
        block = grads[pl.ds(slot, width), :]
        if step == 0:
            kept[...] = block
        for index in range(split):
            packed[index * width : (index + 1) * width, :] = block[:, index * hidden : (index + 1) * hidden]
        messages[step][...] = packed[...].astype(bf16)


def backward(got, weight, band, size):
    members = len(got)
    group = group_of(members)
    order = [0, *range(2, members), 1][:members]
    hidden = weight.shape[0]
    nodes, total = band.shape
    width = hidden // size
    rows = pltpu.VMEM((total // members * group, hidden), bf16)
    early = pl.pallas_call(
        functools.partial(early_kernel, group, members),
        out_shape=struct((hidden, nodes), f32),
        in_specs=[vmem()] * (group + 2),
        out_specs=vmem(),
        scratch_shapes=[rows],
        compiler_params=room(band, *got),
        name="early",
    )(*got[:group], weight, band)
    message = struct((width * (nodes // hidden) + hidden + tail, hidden), bf16)
    return pl.pallas_call(
        functools.partial(backward_kernel, order, size, group, members),
        out_shape=(message,) * size + (struct((width, nodes), f32),),
        in_specs=[vmem()] * (members + 3),
        out_specs=(vmem(),) * (size + 1),
        scratch_shapes=[
            rows,
            pltpu.VMEM((members, hidden, hidden), f32),
            pltpu.VMEM((members, 1, hidden), f32),
            pltpu.VMEM((hidden, nodes), f32),
            pltpu.VMEM(message.shape, f32),
        ],
        compiler_params=room(band, *got),
        name="backward",
    )(*[got[step] for step in order], weight, band, early)


def final_kernel(order, size, shrink, *refs):
    given, (kept, features_out, weight_out, bias_out, slots, features, weight, bias, sems) = refs[:size], refs[size:]
    width, nodes = kept.shape
    hidden = weight.shape[0]
    split = nodes // hidden
    me = lax.axis_index("row")
    messages = [given[order.index(step)] for step in range(size)]
    pairs = ((weight, weight_out), (bias, bias_out), (features, features_out))
    copies = [pltpu.make_async_copy(a, b, sems.at[i]) for i, (a, b) in enumerate(pairs)]
    for step, message in enumerate(messages):
        slots[source(me, step, size)] = message[split * width :, :].astype(f32)
    total = slots[0]
    for index in range(1, size):
        total = total + slots[index]
    weight[...] = total[:hidden] * shrink
    copies[0].start()
    bias[...] = jnp.sum(total[hidden:], axis=0, keepdims=True) * shrink
    copies[1].start()
    for index in range(split):
        place = slice(index * hidden, (index + 1) * hidden)
        total = kept[:, place]
        for message in messages[1:]:
            total = total + message[index * width : (index + 1) * width, :].astype(f32)
        features[:, place] = total.astype(bf16)
    copies[2].start()
    for copy in copies:
        copy.wait()


def final(messages, kept, hidden, shrink):
    width, nodes = kept.shape
    size = len(messages)
    order = [0, *range(size - 1, 0, -1)]
    outs = (struct((width, nodes), bf16), struct((hidden, hidden), f32), struct((1, hidden), f32))
    return pl.pallas_call(
        functools.partial(final_kernel, order, size, shrink),
        out_shape=outs,
        in_specs=[vmem()] * (size + 1),
        out_specs=(pl.BlockSpec(memory_space=pltpu.HBM),) * 3,
        scratch_shapes=[pltpu.VMEM((size, hidden + tail, hidden), f32)]
        + [pltpu.VMEM(out.shape, out.dtype) for out in outs]
        + [pltpu.SemaphoreType.DMA((3,))],
        compiler_params=room(*messages),
        name="final",
    )(*[messages[step] for step in order], kept)


def shards(
    features,
    weight,
    bias_vector,
    tile_rows,
    tile_cols,
    neighbours,
    edge_weights,
    tile_count,
    cotangent,
):
    tile_size = neighbours.shape[-1]
    hidden = weight.shape[1]
    size, owners = lax.axis_size("row"), lax.axis_size("col")
    twins = 2 if owners % 2 == 0 else 1
    members = owners // twins
    blocks_own = cotangent.shape[0] // tile_size
    row_blocks = blocks_own * owners
    col_blocks = blocks_own * size
    turned = features.T
    parts = [turned] + [exchange(turned, "row", step, size) for step in range(1, size)]
    band, bias, longer = make_band(
        tile_count, tile_rows, tile_cols, neighbours, edge_weights, bias_vector, cotangent, row_blocks, col_blocks, members, twins
    )
    kept, *messages = forward(parts, band, members)
    got = [exchange(message, "col", step + 1, members) for step, message in enumerate(messages)]
    cotangents = [cotangent]
    if twins > 1:
        cotangents.append(exchange_twin(longer, "col", members))
    sums = add(kept, got[::-1])
    others = [exchange_twin(sums, "col", members)] if twins > 1 else []
    whole, first, given = before(cotangents, sums, weight, members)
    pre, message = own_rows(whole, first, given, weight, bias, others)
    activations = activate(pre, cotangent.shape[0], members)
    got = [message] + [exchange(message, "col", step, members) for step in range(1, members)]
    *messages, kept = backward(got, weight, band, size)
    messages = [messages[0]] + [exchange(messages[step], "row", step, size) for step in range(1, size)]
    node_count = cotangent.shape[0] * size * owners
    grad_features, grad_weight, grad_bias = final(messages, kept, hidden, float(node_count) ** (-0.5))
    return (activations, grad_features.T, grad_weight, grad_bias.reshape(hidden))


def solution(mesh):
    in_specs = (
        P("col", "row"),
        P(),
        P(),
        P("row", "col", None),
        P("row", "col", None),
        P("row", "col", None, None, None),
        P("row", "col", None, None, None),
        P("row", "col"),
        P(("row", "col"), None),
    )
    out_specs = (P(("row", "col"), None), P("col", "row"), P(), P())
    return jax.shard_map(shards, mesh=mesh, in_specs=in_specs, out_specs=out_specs, check_vma=False)
```

```python
import functools

import jax
import jax.numpy as jnp
from jax import lax
from jax.experimental import pallas as pl
from jax.experimental.pallas import tpu as pltpu
from jax.sharding import PartitionSpec as P

f32 = jnp.float32
bf16 = jnp.bfloat16
i16 = jnp.int16
levels = 32736.0
tail = 16
wide = 1024
grant = 8 * 2**20


def room(*arrays):
    size = sum(a.size * a.dtype.itemsize for a in arrays)
    return pltpu.CompilerParams(vmem_limit_bytes=grant + 2 * size)


def vmem():
    return pl.BlockSpec(memory_space=pltpu.VMEM)


def smem():
    return pl.BlockSpec(memory_space=pltpu.SMEM)


def struct(shape, dtype):
    return jax.ShapeDtypeStruct(shape, dtype)


def dims(left, right):
    return (((left,), (right,)), ((), ()))


def dot(a, b, left=1, right=0):
    return lax.dot_general(a, b, dims(left, right), preferred_element_type=f32)


def each(count, body):
    if count <= 64:
        for index in range(count):
            body(index)
    else:
        lax.fori_loop(0, count, lambda index, none: (body(index), none)[1], 0)


def start_of(index, size):
    return index * size if isinstance(index, int) else pl.multiple_of(index * size, size)


def code(value, out):
    rows = value.shape[0]
    top = jnp.max(jnp.abs(value), axis=0, keepdims=True)
    power = jnp.ceil(jnp.log2(jnp.maximum(top, 1e-20)))
    out[:rows, :] = jnp.round(value * (jnp.exp2(-power) * levels)).astype(jnp.int32).astype(i16)
    out[rows:, :] = jnp.broadcast_to(power, (tail, value.shape[1])).astype(jnp.int32).astype(i16)


def decode(part):
    whole = part[...].astype(jnp.int32).astype(f32)
    rows = whole.shape[0] - tail
    return whole[:rows] * (jnp.exp2(whole[rows : rows + 1]) * (1.0 / levels))


def partner(me, step, size):
    if size & (size - 1) == 0:
        return me ^ step
    return (me + step) % size


def source(me, step, size):
    if size & (size - 1) == 0:
        return me ^ step
    return (me + size - step) % size


def exchange(value, axis, step, members):
    size = lax.axis_size(axis)
    pairs = [(i, i // members * members + partner(i % members, step, members)) for i in range(size)]
    return lax.ppermute(value, axis, pairs)


def exchange_twin(value, axis, members):
    size = lax.axis_size(axis)
    return lax.ppermute(value, axis, [(i, (i + members) % size) for i in range(size)])


def band_kernel(
    place, limit, rows, cols, ids, values, bias, cotangent, band, bias_out, longer, sums, scaled, here, row, col, sems
):
    blocks, tile, _ = sums.shape
    row_blocks = band.shape[1] // tile
    slots = rows.shape[-1]
    ids_here, values_here = here
    lanes = ids_here.shape[0] // slots
    pairs = ((ids, ids_here), (values, values_here), (rows, row), (cols, col), (bias, bias_out))
    pairs = pairs + ((cotangent, longer.at[pl.ds(0, cotangent.shape[0]), :]),)
    copies = [pltpu.make_async_copy(a, b, sems.at[i]) for i, (a, b) in enumerate(pairs)]
    for copy in copies:
        copy.start()
    longer[cotangent.shape[0] :, :] = jnp.zeros((tail, cotangent.shape[1]), f32)

    def clear(index):
        sums[index] = jnp.zeros((tile, tile), f32)

    each(blocks, clear)
    for copy in copies:
        copy.wait()
    line = lax.broadcasted_iota(jnp.int32, scaled.shape, 0)
    scaled[...] = jnp.where(line < limit[0, 0] * lanes, values_here[...].astype(f32), 0.0)
    which = lax.broadcasted_iota(jnp.int32, (tile, tile), 0)

    def add(slot):
        block = col[0, 0, slot] * row_blocks + row[0, 0, slot]
        dense = jnp.zeros((tile, tile), f32)
        for lane in range(lanes):
            place = pl.ds(slot * lanes + lane, 1)
            dense = jnp.where(which == ids_here[place, :], scaled[place, :], dense)
        sums[block] = sums[block] + dense

    several = next(count for count in (4, 2, 1) if slots % count == 0)

    def group(index, none):
        for other in range(several):
            add(index * several + other)
        return none

    lax.fori_loop(0, (limit[0, 0] + several - 1) // several, group, 0)

    def put(index):
        c, r = index // row_blocks, place(index % row_blocks)
        band[pl.ds(start_of(c, tile), tile), pl.ds(start_of(r, tile), tile)] = sums[index].astype(bf16)

    each(blocks, put)


def make_band(limit, rows, cols, ids, values, bias, cotangent, row_blocks, col_blocks, members, twins):
    blocks_own = row_blocks // (members * twins)

    def place(block):
        owner = block // blocks_own
        return (owner % members * twins + owner // members) * blocks_own + block % blocks_own

    tile = ids.shape[-1]
    lines = ids.shape[-3] * ids.shape[-2]
    ids = ids.reshape(lines, tile)
    values = values.reshape(lines, tile)
    bias = bias.reshape(1, -1)
    out = struct((col_blocks * tile, row_blocks * tile), bf16)
    sums = struct((col_blocks * row_blocks, tile, tile), f32)
    return pl.pallas_call(
        functools.partial(band_kernel, place),
        out_shape=(out, struct(bias.shape, f32), struct((cotangent.shape[0] + tail, cotangent.shape[1]), f32)),
        in_specs=[smem()] + [pl.BlockSpec(memory_space=pltpu.HBM)] * 6,
        out_specs=(vmem(),) * 3,
        scratch_shapes=[
            pltpu.VMEM(sums.shape, f32),
            pltpu.VMEM((lines, tile), f32),
            (pltpu.VMEM((lines, tile), jnp.int32), pltpu.VMEM((lines, tile), bf16)),
            pltpu.SMEM(rows.shape, jnp.int32),
            pltpu.SMEM(cols.shape, jnp.int32),
            pltpu.SemaphoreType.DMA((6,)),
        ],
        compiler_params=pltpu.CompilerParams(vmem_limit_bytes=grant + sums.size * 4 + out.size * 2),
        cost_estimate=pl.CostEstimate(flops=8 * sums.size * 8, bytes_accessed=8 * 2**20, transcendentals=0),
        name="band",
    )(limit, *[pltpu.with_memory_space_constraint(a, pltpu.HBM) for a in (rows, cols, ids, values, bias, cotangent)])


def forward_kernel(size, members, *refs):
    parts, (band, kept), messages, panel = refs[:size], refs[size : size + 2], refs[size + 2 : -1], refs[-1]
    me = lax.axis_index("row")
    mine = lax.rem(lax.axis_index("col"), members)
    width = parts[0].shape[0]
    own = kept.shape[1]
    for step, part in enumerate(parts):
        slot = pl.multiple_of(source(me, step, size) * width, width)
        panel[pl.ds(slot, width), :] = part[...].astype(panel.dtype)
    left = panel[...].astype(bf16)
    for step, message in enumerate((kept,) + messages):
        columns = pl.ds(pl.multiple_of(partner(mine, step, members) * own, own), own)
        got = dot(left, band[:, columns])
        if step == 0:
            kept[...] = got
        else:
            code(got, message)


def forward(parts, band, members):
    width = parts[0].shape[0]
    hidden = width * len(parts)
    nodes, total = band.shape
    block = (hidden, total // members)
    panel = pltpu.VMEM((hidden, nodes), bf16 if width % 16 == 0 else f32)
    return pl.pallas_call(
        functools.partial(forward_kernel, len(parts), members),
        out_shape=(struct(block, f32),) + (struct((hidden + tail, block[1]), i16),) * (members - 1),
        in_specs=[vmem()] * (len(parts) + 1),
        out_specs=(vmem(),) * members,
        scratch_shapes=[panel],
        compiler_params=room(band),
        name="forward",
    )(*parts, band)


def add_kernel(kept, *refs):
    parts, out = refs[:-1], refs[-1]
    total = kept[...]
    for part in parts:
        total = total + decode(part)
    code(total, out)


def add(kept, parts):
    return pl.pallas_call(
        add_kernel,
        out_shape=struct((kept.shape[0] + tail, kept.shape[1]), i16),
        in_specs=[vmem()] * (len(parts) + 1),
        out_specs=vmem(),
        compiler_params=room(kept),
        name="add",
    )(kept, *parts)


def pair_rows(line):
    high = line.astype(bf16).astype(f32)
    row = lax.broadcasted_iota(jnp.int32, (tail, line.shape[1]), 0)
    return jnp.where(row == 0, high, jnp.where(row == 1, line - high, 0.0))


def parts_of(value):
    high = value.astype(bf16)
    return high, (value - high.astype(f32)).astype(bf16)


def apply(value, weight):
    high, low = parts_of(value)
    return dot(high, weight[...], 0, 0) + dot(low, weight[...], 0, 0)


def before_kernel(members, twins, *refs):
    cotangents, (sums, weight, whole, first, given) = refs[:twins], refs[twins:]
    mine = lax.axis_index("col") // members
    own = cotangents[0].shape[0]
    for index, part in enumerate(cotangents):
        place = mine if index == 0 else twins - 1 - mine
        given[pl.ds(pl.multiple_of(place * own, own), own), :] = part[:own, :]
    value = decode(sums)
    whole[...] = value
    first[...] = apply(value, weight)


def before(cotangents, sums, weight, members):
    hidden, rows = sums.shape[0] - tail, sums.shape[1]
    product = struct((rows, weight.shape[1]), f32)
    return pl.pallas_call(
        functools.partial(before_kernel, members, len(cotangents)),
        out_shape=(struct((hidden, rows), f32), product, product),
        in_specs=[vmem()] * (len(cotangents) + 2),
        out_specs=(vmem(),) * 3,
        compiler_params=room(sums),
        name="before",
    )(*cotangents, sums, weight)


def own_kernel(weight, bias, whole, first, given, *refs):
    others, (pre_out, message) = refs[:-2], refs[-2:]
    total, pre = whole[...], first[...]
    for part in others:
        value = decode(part)
        total = total + value
        pre = pre + apply(value, weight)
    pre = pre + bias[...]
    pre_out[...] = pre
    squashed = jax.nn.sigmoid(pre)
    grad = given[...] * squashed * (1.0 + pre * (1.0 - squashed))
    grad = grad.astype(bf16)
    rows = grad.shape[0]
    message[:rows, :] = grad
    high, low = parts_of(total)
    message[rows:, :] = (dot(high, grad) + dot(low, grad)).astype(bf16)


def own_rows(whole, first, given, weight, bias, others):
    hidden, rows = whole.shape
    return pl.pallas_call(
        own_kernel,
        out_shape=(struct((rows, hidden), f32), struct((rows + hidden, hidden), bf16)),
        in_specs=[vmem()] * (5 + len(others)),
        out_specs=(vmem(),) * 2,
        compiler_params=room(whole),
        name="own_rows",
    )(weight, bias, whole, first, given, *others)


def activate_kernel(members, pre, act):
    own = act.shape[0]
    mine = lax.axis_index("col") // members
    kept = pre[pl.ds(pl.multiple_of(mine * own, own), own), :]
    act[...] = kept * jax.nn.sigmoid(kept)


def activate(pre, own, members):
    return pl.pallas_call(
        functools.partial(activate_kernel, members),
        out_shape=struct((own, pre.shape[1]), f32),
        in_specs=[vmem()],
        out_specs=vmem(),
        compiler_params=room(pre),
        name="activate",
    )(pre)


def group_of(members):
    return 2 if members % 2 == 0 and members & (members - 1) == 0 else 1


def group_product(parts, first, weight, band, rows, mine, members):
    group = len(parts)
    own = rows.shape[0] // group
    base = source(mine, first, members) // group * group
    for index, part in enumerate(parts):
        spot = pl.multiple_of((source(mine, first + index, members) - base) * own, own)
        rows[pl.ds(spot, own), :] = part[:own, :]
    back = dot(weight[...], rows[...], 1, 1).astype(bf16)
    wide_own = group * own
    return dot(back, band[:, pl.ds(pl.multiple_of(base * own, wide_own), wide_own)], 1, 1)


def early_kernel(group, members, *refs):
    parts, (weight, band, out, rows) = refs[:group], refs[group:]
    mine = lax.rem(lax.axis_index("col"), members)
    out[...] = group_product(parts, 0, weight, band, rows, mine, members)


def backward_kernel(order, size, group, members, *refs):
    given, (weight, band, early), messages = refs[:members], refs[members : members + 3], refs[members + 3 :][:size]
    kept, rows, slots, lines, grads, packed = refs[members + 3 + size :]
    got = [given[order.index(step)] for step in range(members)]
    hidden = weight.shape[0]
    own = got[0].shape[0] - hidden
    width, nodes = kept.shape
    me = lax.axis_index("row")
    mine = lax.rem(lax.axis_index("col"), members)
    for step, part in enumerate(got):
        place = source(mine, step, members)
        slots[place] = part[own:, :].astype(f32)
        lines[place] = jnp.sum(part[:own, :].astype(f32), axis=0, keepdims=True)
    weight_part, bias_part = slots[0], lines[0]
    for index in range(1, members):
        weight_part = weight_part + slots[index]
        bias_part = bias_part + lines[index]
    total = early[...]
    for first in range(group, members, group):
        total = total + group_product(got[first : first + group], first, weight, band, rows, mine, members)
    grads[...] = total
    split = nodes // hidden
    packed[split * width : split * width + hidden, :] = weight_part
    packed[split * width + hidden :, :] = pair_rows(bias_part)
    for step in range(size):
        slot = pl.multiple_of(partner(me, step, size) * width, width)
        block = grads[pl.ds(slot, width), :]
        if step == 0:
            kept[...] = block
        for index in range(split):
            packed[index * width : (index + 1) * width, :] = block[:, index * hidden : (index + 1) * hidden]
        messages[step][...] = packed[...].astype(bf16)


def backward(got, weight, band, size):
    members = len(got)
    group = group_of(members)
    order = [0, *range(2, members), 1][:members]
    hidden = weight.shape[0]
    nodes, total = band.shape
    width = hidden // size
    rows = pltpu.VMEM((total // members * group, hidden), bf16)
    early = pl.pallas_call(
        functools.partial(early_kernel, group, members),
        out_shape=struct((hidden, nodes), f32),
        in_specs=[vmem()] * (group + 2),
        out_specs=vmem(),
        scratch_shapes=[rows],
        compiler_params=room(band, *got),
        name="early",
    )(*got[:group], weight, band)
    message = struct((width * (nodes // hidden) + hidden + tail, hidden), bf16)
    return pl.pallas_call(
        functools.partial(backward_kernel, order, size, group, members),
        out_shape=(message,) * size + (struct((width, nodes), f32),),
        in_specs=[vmem()] * (members + 3),
        out_specs=(vmem(),) * (size + 1),
        scratch_shapes=[
            rows,
            pltpu.VMEM((members, hidden, hidden), f32),
            pltpu.VMEM((members, 1, hidden), f32),
            pltpu.VMEM((hidden, nodes), f32),
            pltpu.VMEM(message.shape, f32),
        ],
        compiler_params=room(band, *got),
        name="backward",
    )(*[got[step] for step in order], weight, band, early)


def final_kernel(order, size, shrink, *refs):
    given, (kept, features_out, weight_out, bias_out, slots, features, weight, bias, sems) = refs[:size], refs[size:]
    width, nodes = kept.shape
    hidden = weight.shape[0]
    split = nodes // hidden
    me = lax.axis_index("row")
    messages = [given[order.index(step)] for step in range(size)]
    pairs = ((weight, weight_out), (bias, bias_out), (features, features_out))
    copies = [pltpu.make_async_copy(a, b, sems.at[i]) for i, (a, b) in enumerate(pairs)]
    for step, message in enumerate(messages):
        slots[source(me, step, size)] = message[split * width :, :].astype(f32)
    total = slots[0]
    for index in range(1, size):
        total = total + slots[index]
    weight[...] = total[:hidden] * shrink
    copies[0].start()
    bias[...] = jnp.sum(total[hidden:], axis=0, keepdims=True) * shrink
    copies[1].start()
    for index in range(split):
        place = slice(index * hidden, (index + 1) * hidden)
        total = kept[:, place]
        for message in messages[1:]:
            total = total + message[index * width : (index + 1) * width, :].astype(f32)
        features[:, place] = total.astype(bf16)
    copies[2].start()
    for copy in copies:
        copy.wait()


def final(messages, kept, hidden, shrink):
    width, nodes = kept.shape
    size = len(messages)
    order = [0, *range(size - 1, 0, -1)]
    outs = (struct((width, nodes), bf16), struct((hidden, hidden), f32), struct((1, hidden), f32))
    return pl.pallas_call(
        functools.partial(final_kernel, order, size, shrink),
        out_shape=outs,
        in_specs=[vmem()] * (size + 1),
        out_specs=(pl.BlockSpec(memory_space=pltpu.HBM),) * 3,
        scratch_shapes=[pltpu.VMEM((size, hidden + tail, hidden), f32)]
        + [pltpu.VMEM(out.shape, out.dtype) for out in outs]
        + [pltpu.SemaphoreType.DMA((3,))],
        compiler_params=room(*messages),
        name="final",
    )(*[messages[step] for step in order], kept)


def shards(
    features,
    weight,
    bias_vector,
    tile_rows,
    tile_cols,
    neighbours,
    edge_weights,
    tile_count,
    cotangent,
):
    tile_size = neighbours.shape[-1]
    hidden = weight.shape[1]
    size, owners = lax.axis_size("row"), lax.axis_size("col")
    twins = 2 if owners % 2 == 0 else 1
    members = owners // twins
    blocks_own = cotangent.shape[0] // tile_size
    row_blocks = blocks_own * owners
    col_blocks = blocks_own * size
    turned = features.T
    parts = [turned] + [exchange(turned, "row", step, size) for step in range(1, size)]
    band, bias, longer = make_band(
        tile_count, tile_rows, tile_cols, neighbours, edge_weights, bias_vector, cotangent, row_blocks, col_blocks, members, twins
    )
    kept, *messages = forward(parts, band, members)
    got = [exchange(message, "col", step + 1, members) for step, message in enumerate(messages)]
    cotangents = [cotangent]
    if twins > 1:
        cotangents.append(exchange_twin(longer, "col", members))
    sums = add(kept, got[::-1])
    others = [exchange_twin(sums, "col", members)] if twins > 1 else []
    whole, first, given = before(cotangents, sums, weight, members)
    pre, message = own_rows(whole, first, given, weight, bias, others)
    activations = activate(pre, cotangent.shape[0], members)
    got = [message] + [exchange(message, "col", step, members) for step in range(1, members)]
    *messages, kept = backward(got, weight, band, size)
    messages = [messages[0]] + [exchange(messages[step], "row", step, size) for step in range(1, size)]
    node_count = cotangent.shape[0] * size * owners
    grad_features, grad_weight, grad_bias = final(messages, kept, hidden, float(node_count) ** (-0.5))
    return (activations, grad_features.T, grad_weight, grad_bias.reshape(hidden))


def solution(mesh):
    in_specs = (
        P("col", "row"),
        P(),
        P(),
        P("row", "col", None),
        P("row", "col", None),
        P("row", "col", None, None, None),
        P("row", "col", None, None, None),
        P("row", "col"),
        P(("row", "col"), None),
    )
    out_specs = (P(("row", "col"), None), P("col", "row"), P(), P())
    return jax.shard_map(shards, mesh=mesh, in_specs=in_specs, out_specs=out_specs, check_vma=False)
```
